256 devices in a mesh: dom: 64 (over z, x, core), grp: 4 (over y).
Axes of the slice: x: 4, y: 4, z: 8, core: 2. Of those that a mesh axis runs over, the one named last changes fastest.
Arguments:
- features: bfloat16 [262144, 512], P(('dom', 'grp')), may hold values from -6 to 6
- tile_src: int32 [2048, 8], P(('dom', 'grp')), may hold values from 0 to 15
- tile_val: bfloat16 [2048, 8, 128, 128], P(('dom', 'grp')), may hold values from -0.1875 to 0.1875
- send_sel: int32 [256, 64], P(('dom', 'grp')), may hold values from 0 to 63
- stale_features: bfloat16 [262144, 512], P(('dom', 'grp')), may hold values from -5 to 5
- stale_grads: bfloat16 [262144, 512], P(('dom', 'grp')), may hold values from -6 to 6
- out_grad: bfloat16 [262144, 512], P(('dom', 'grp')), may hold values from -6 to 6
- master: float32 [2, 512, 512], P(None, ('dom', 'grp')), may hold values from -0.25 to 0.25
- moment_first: float32 [2, 512, 512], P(None, ('dom', 'grp')), may hold values from -0.0078125 to 0.0078125
- moment_second: float32 [2, 512, 512], P(None, ('dom', 'grp')), may hold values from 7.6293944e-08 to 1.9073486e-06
Outputs:
- layer_out: bfloat16 [262144, 512], P(('dom', 'grp'))
- fresh_features: bfloat16 [262144, 512], P(('dom', 'grp'))
- fresh_grads: bfloat16 [262144, 512], P(('dom', 'grp'))
- master_next: float32 [2, 512, 512], P(None, ('dom', 'grp'))
- weights_next: bfloat16 [2, 512, 512], replicated
The draws below stay inside these ranges and needn't reach their ends.
Inputs may be any that keep to these rules, and one draw needn't show every extreme that they name: `tile_src`: A value below 8 names a local row block; 8 + b names boundary block b.
All inputs are finite; a program needn't handle non-finite values.
Results may differ from the reference program's by a relative error of at most 0.005.
The reference program's roundings to bfloat16 on the way count: a program that leaves them out, or rounds other values in their place, can miss the bound.
Values may be sent and summed in bfloat16 or wider, within the bound.
A program may use at most 128 MiB of HBM per device.

```python
import math
import jax
import jax.numpy as jnp
from jax import lax

F = 512
BLOCK = 128
TILES = 8
PIECE = 16
STEP = 10
RB = 8
NODES_DEV = 1024
TOTAL_NODES = 262144
ALL_BLOCKS = 2048
ALL_RIM = 262144
N_DOM = 64
N_GRP = 4


def with_ends(drawn, stream_key, low, high):
    index_at = [jax.random.randint(jax.random.fold_in(stream_key, axis), (), 0, length) for axis, length in enumerate(drawn.shape)]
    longest = drawn.shape.index(max(drawn.shape))
    beside = index_at[:longest] + [(index_at[longest] + 1) % drawn.shape[longest]] + index_at[longest + 1:]
    return drawn.at[tuple(index_at)].set(low).at[tuple(beside)].set(high)


def level_of(key, extent, split, smallest, top_value):
    gain = 1.0
    for axis_at, blocks in split:
        steps = jax.random.uniform(jax.random.fold_in(jax.random.fold_in(key, 6), axis_at), (blocks,), jnp.float32, smallest / len(split), top_value / len(split))
        gain = gain * jnp.repeat(jnp.exp(steps), extent[axis_at] // blocks).reshape((-1,) + (1,) * (len(extent) - 1 - axis_at))
    return gain


def gaussian(key, extent, scale, bound, cuts=(), kind=jnp.bfloat16):
    factor_of = level_of(key, extent, cuts, -0.22, 0.18) if cuts else 1.0
    array = jax.random.normal(key, extent, jnp.float32) * scale * factor_of
    return jnp.minimum(jnp.maximum(array, -bound), bound).astype(kind)


def setup_inputs(seed: int = 0) -> dict:
    key_list = jax.random.split(jax.random.key(seed), 11)
    features = gaussian(key_list[0], (TOTAL_NODES, F), 1.0, 6.0, ((0, 256),))
    tile_src = with_ends(jax.random.randint(key_list[1], (ALL_BLOCKS, TILES), 0, RB + N_DOM * PIECE // BLOCK), jax.random.fold_in(key_list[1], 1), 0, (RB + N_DOM * PIECE // BLOCK) - 1).astype(jnp.int32)
    tile_val = gaussian(key_list[2], (ALL_BLOCKS, TILES, BLOCK, BLOCK), (TILES * BLOCK) ** -0.5, 0.1875, ((0, 256),))
    send_sel = with_ends(jax.random.randint(key_list[3], (N_DOM * N_GRP, N_DOM), 0, NODES_DEV // PIECE), jax.random.fold_in(key_list[3], 1), 0, (NODES_DEV // PIECE) - 1).astype(jnp.int32)
    stale_features = gaussian(key_list[4], (ALL_RIM, F), 0.7, 5.0, ((0, 256),))
    stale_grads = gaussian(key_list[5], (ALL_RIM, F), 1.0, 6.0, ((0, 256),))
    out_grad = gaussian(key_list[6], (TOTAL_NODES, F), 1.0, 6.0, ((0, 256),))
    master = gaussian(key_list[7], (2, F, F), F ** -0.5, 0.25, ((1, 256),), jnp.float32)
    moment_first = gaussian(key_list[8], (2, F, F), (0.3 / TOTAL_NODES ** 0.5), 0.0078125, ((1, 256),), jnp.float32)
    moment_second = jnp.clip(jnp.exp(math.log(1.9073486328125e-06) - 3.218876 * jax.random.uniform(key_list[9], (2, F, F), jnp.float32) ** level_of(key_list[9], (2, F, F), ((1, 256),), -0.2, 0.2)), 7.629394360719743e-08, 1.9073486328125e-06)
    return dict(features=features, tile_src=tile_src, tile_val=tile_val, send_sel=send_sel, stale_features=stale_features, stale_grads=stale_grads, out_grad=out_grad, master=master, moment_first=moment_first, moment_second=moment_second)


decay_first = 0.9
decay_second = 0.95
learn_rate = 0.01
epsilon = 1e-08

def aggregate(local_rows, rim_rows, tile_block, sources):
    lookup = jnp.concatenate([local_rows, rim_rows], 0).reshape(-1, BLOCK, F)
    picked = lookup[sources]
    total = jnp.einsum('rtij,rtjf->rif', tile_block.astype(jnp.float32), picked.astype(jnp.float32))
    return total.reshape(-1, F)

def spread(tile_block, sources, upstream):
    contrib = jnp.einsum('rtij,rif->rtjf', tile_block.astype(jnp.float32), upstream.reshape(RB, BLOCK, F).astype(jnp.float32))
    slots = RB + N_DOM * PIECE // BLOCK
    onehot = (sources.reshape(-1)[:, None] == jnp.arange(slots, dtype=jnp.int32)[None, :]).astype(jnp.float32)
    total = jnp.einsum('kb,kjf->bjf', onehot, contrib.reshape(RB * TILES, BLOCK, F), precision=lax.Precision.HIGHEST)
    return total.reshape(-1, F)

def swap_peers(pieces):
    return pieces.reshape(N_DOM, N_GRP, N_DOM, PIECE, F).transpose(2, 1, 0, 3, 4).reshape(-1, F)

def reference(features, tile_src, tile_val, send_sel, stale_features, stale_grads, out_grad, master, moment_first, moment_second):
    devices = N_DOM * N_GRP
    weights = master.astype(jnp.bfloat16)
    selects = send_sel.reshape(devices, N_DOM)
    tile_blocks = tile_val.reshape(devices, RB, TILES, BLOCK, BLOCK)
    source_ids = tile_src.reshape(devices, RB, TILES)

    def outgoing(node_rows):
        pieces = node_rows.reshape(devices, -1, PIECE, F)
        chosen = jax.vmap(lambda group, picks: group[picks])(pieces, selects)
        return swap_peers(chosen.reshape(-1, F))

    def aggregate_all(node_rows, rim_all):
        packs = (node_rows.reshape(devices, RB * BLOCK, F), rim_all.reshape(devices, N_DOM * PIECE, F), tile_blocks, source_ids)
        return lax.map(lambda packed: aggregate(packed[0], packed[1], packed[2], packed[3]), packs).reshape(-1, F)
    p_first = aggregate_all(features, outgoing(features)).astype(jnp.bfloat16)
    z_first = jnp.dot(p_first, weights[0], preferred_element_type=jnp.float32)
    h_first = jax.nn.silu(z_first).astype(jnp.bfloat16)
    fresh_features = outgoing(h_first)
    p_second = aggregate_all(h_first, stale_features).astype(jnp.bfloat16)
    layer_out = jnp.dot(p_second, weights[1], preferred_element_type=jnp.float32).astype(jnp.bfloat16)
    upstream = jnp.dot(out_grad, weights[1].T, preferred_element_type=jnp.float32).astype(jnp.bfloat16)
    g_second = jnp.dot(p_second.T, out_grad, preferred_element_type=jnp.float32) / TOTAL_NODES
    packs = (tile_blocks, source_ids, upstream.reshape(devices, RB * BLOCK, F))
    spreads = lax.map(lambda packed: spread(packed[0], packed[1], packed[2]), packs)
    local_part = spreads[:, :RB * BLOCK]
    fresh_grads = swap_peers(spreads[:, RB * BLOCK:].astype(jnp.bfloat16).reshape(-1, F))
    piece_count = RB * BLOCK // PIECE
    placing = (selects[:, :, None] == jnp.arange(piece_count, dtype=jnp.int32)[None, None, :]).astype(jnp.float32)
    stale_slots = stale_grads.reshape(devices, N_DOM, PIECE, F).astype(jnp.float32)
    placed = jnp.einsum('dpq,dprf->dqrf', placing, stale_slots, precision=lax.Precision.HIGHEST)
    d_first = (local_part + placed.reshape(devices, -1, F)).reshape(-1, F)
    sigma = jax.nn.sigmoid(z_first)
    dz = (d_first * sigma * (1.0 + z_first * (1.0 - sigma))).astype(jnp.bfloat16)
    g_first = jnp.dot(p_first.T, dz, preferred_element_type=jnp.float32) / TOTAL_NODES
    grads = jnp.stack([g_first, g_second])
    moment_new = decay_first * moment_first + (1.0 - decay_first) * grads
    second_new = decay_second * moment_second + (1.0 - decay_second) * grads * grads
    update = moment_new / (1.0 - decay_first ** STEP) / (jnp.sqrt(second_new / (1.0 - decay_second ** STEP)) + epsilon)
    master_next = master - learn_rate * update
    weights_next = master_next.astype(jnp.bfloat16)
    return (layer_out, fresh_features, fresh_grads, master_next, weights_next)
```

```python
import functools

import jax
import jax.numpy as jnp
from jax import lax
from jax.experimental import pallas as pl
from jax.experimental.pallas import tpu as pltpu
from jax.sharding import Mesh
from jax.sharding import PartitionSpec as P

STEP = 10
DEVICES = ("z", "x", "c", "y")
NZ, NX, NC, NY = 8, 4, 2, 4
PEERS = NZ * NX * NC
F = 512
NODES = 1024
PIECE = 16
TOTAL_NODES = 262144
MESH = pl.DeviceIdType.MESH
BF16 = jnp.bfloat16
F32 = jnp.float32

decay_first = 0.9
decay_second = 0.95
learn_rate = 0.01
epsilon = 1e-08


def dot(a, b):
    return jnp.dot(a, b, preferred_element_type=F32)


def dot_over_rows(a, b):
    return lax.dot_general(a, b, (((0,), (0,)), ((), ())), preferred_element_type=F32)


def dot_over_columns(a, b):
    return lax.dot_general(a, b, (((1,), (1,)), ((), ())), preferred_element_type=F32)


def rows_of(index, count):
    return pl.ds(pl.multiple_of(index * count, count), count)


def repeat(count, body):
    def step(i, carry):
        body(i)
        return carry

    lax.fori_loop(0, count, step, 0)


def kernel(
    src_ref,
    sel_row_ref,
    master_ref,
    first_ref,
    second_ref,
    features_hbm,
    tiles_hbm,
    stale_features_hbm,
    stale_grads_hbm,
    out_grad_hbm,
    layer_out_hbm,
    fresh_features_hbm,
    fresh_grads_hbm,
    master_next_ref,
    weights_next_hbm,
    features,
    rim,
    tiles,
    dense,
    out_grad,
    stale_features,
    stale_grads,
    raw_send,
    feature_send,
    grad_send,
    upstream,
    p_local,
    p_stale,
    d_first,
    p_first,
    dz,
    hidden,
    p_second,
    layer_out,
    weights,
    weights_next,
    gather_now,
    gather_next,
    grad_blocks,
    from_core,
    core_sum,
    from_y,
    y_sum,
    from_plane,
    shard_now,
    shard_next,
    rows_f32,
    src_wide,
    want_down,
    choose,
    perm,
    perm_back,
    load_sem,
    store_sem,
    send_sem,
    recv_sem,
):
    z, x, c, y = (lax.axis_index(a) for a in DEVICES)
    plane = z * NX + x
    me = plane * NC + c

    loads = [
        pltpu.make_async_copy(s, d, load_sem.at[i])
        for i, (s, d) in enumerate(
            (
                (features_hbm, features),
                (tiles_hbm, tiles),
                (out_grad_hbm, out_grad),
                (stale_grads_hbm, stale_grads),
                (stale_features_hbm, stale_features),
            )
        )
    ]
    for load in loads:
        load.start()

    def peer_at(step):
        dz_, dx_, dc_ = step // 8, (step // 2) % 4, step % 2
        return ((z + dz_) % NZ, (x + dx_) % NX, (c + dc_) % NC)

    def plane_at(step):
        return ((z + step // 4) % NZ, (x + step % 4) % NX)

    barrier = pltpu.get_barrier_semaphore()

    def greet(i):
        pz, px, pc = peer_at(i + 1)
        pl.semaphore_signal(barrier, inc=1, device_id=(pz, px, pc, y), device_id_type=MESH)

    repeat(PEERS - 1, greet)
    for k in range(1, NY):
        pl.semaphore_signal(
            barrier, inc=1, device_id=(z, x, c, (y + k) % NY), device_id_type=MESH
        )

    def fill_rows(target, source):
        for m in range(2):
            for r in range(2):
                for j in range(4):
                    s = m * 8 + r * 4 + j
                    target[s : s + 1, :] = source[m, r : r + 1, j * 128 : (j + 1) * 128]

    fill_rows(rows_f32.at[0], master_ref)
    fill_rows(rows_f32.at[1], first_ref)
    fill_rows(rows_f32.at[2], second_ref)
    shard_now[...] = rows_f32[0].astype(BF16)

    def bits(o):
        m, j, p = o >> 7, (o >> 5) & 3, (o >> 4) & 1
        return (((o >> 3) & 1) << 7) | (((o >> 1) & 3) << 5) | (p << 4) | (m << 3) | ((o & 1) << 2) | j

    down = lax.broadcasted_iota(jnp.int32, (256, 256), 0)
    along = lax.broadcasted_iota(jnp.int32, (256, 256), 1)
    perm[...] = (bits(down) == along).astype(F32).astype(BF16)
    perm_back[...] = (bits(along) == down).astype(F32).astype(BF16)

    slot_of = lax.broadcasted_iota(jnp.int32, (PEERS, NODES), 1) // PIECE
    slot_at = lax.broadcasted_iota(jnp.int32, (PEERS, NODES), 0)
    widen = (slot_of == slot_at).astype(F32).astype(BF16)
    picks = jnp.broadcast_to(sel_row_ref[...].astype(F32), (16, PEERS)).astype(BF16)
    wide = dot(picks, widen)[0:1, :].astype(jnp.int32)
    lane = lax.broadcasted_iota(jnp.int32, (1, NODES), 1) % PIECE
    wanted = wide * PIECE + lane

    tall = dot_over_rows(widen, dot_over_rows(picks, jnp.full((16, 128), 0.0625, BF16)).astype(BF16))
    want_down[...] = tall.astype(jnp.int32) * PIECE + (
        lax.broadcasted_iota(jnp.int32, (NODES, 128), 0) % PIECE
    )

    def choose_rows(i):
        rows = rows_of(i, 256)
        for k in range(8):
            column = lax.broadcasted_iota(jnp.int32, (256, 128), 1) + k * 128
            chosen = (want_down[rows, :] == column).astype(F32).astype(BF16)
            choose[rows, k * 128 : (k + 1) * 128] = chosen

    repeat(4, choose_rows)

    pl.semaphore_wait(barrier, PEERS - 1 + NY - 1)

    def spread_shard(slot, shard, gathered):
        gathered[c, y, rows_of(plane, 16), :] = shard[...]

        def send(i):
            pz, px = plane_at(i + 1)
            pltpu.make_async_remote_copy(
                src_ref=shard,
                dst_ref=gathered.at[c, y, rows_of(plane, 16)],
                send_sem=send_sem.at[slot],
                recv_sem=recv_sem.at[slot],
                device_id=(pz, px, c, y),
                device_id_type=MESH,
            ).start()

        repeat(NZ * NX - 1, send)

    def plane_bytes(slot, ref):
        return pltpu.make_async_remote_copy(
            src_ref=ref,
            dst_ref=ref,
            send_sem=send_sem.at[slot],
            recv_sem=recv_sem.at[slot],
            device_id=(z, x, c, (y + 1) % NY),
            device_id_type=MESH,
        )

    def gather_y(slot, gathered):
        plane_bytes(slot, gathered.at[0, 0, pl.ds(0, 496)]).wait_recv()
        copies = [
            pltpu.make_async_remote_copy(
                src_ref=gathered.at[c, y],
                dst_ref=gathered.at[c, y],
                send_sem=send_sem.at[slot + 1],
                recv_sem=recv_sem.at[slot + 1],
                device_id=(z, x, c, (y + k) % NY),
                device_id_type=MESH,
            )
            for k in range(1, NY)
        ]
        for copy in copies:
            copy.start()

    def gather_core(slot, gathered):
        plane_bytes(slot + 1, gathered.at[0, pl.ds(0, 3)]).wait_recv()
        pltpu.make_async_remote_copy(
            src_ref=gathered.at[c],
            dst_ref=gathered.at[c],
            send_sem=send_sem.at[slot + 2],
            recv_sem=recv_sem.at[slot + 2],
            device_id=(z, x, 1 - c, y),
            device_id_type=MESH,
        ).start()

    def gather_end(slot, gathered, whole):
        plane_bytes(slot + 2, gathered.at[0]).wait_recv()

        def lay(chunk):
            taken = jnp.concatenate(
                [gathered[a // 4, a % 4, rows_of(chunk, 32), :] for a in range(8)], 0
            )
            laid = dot(perm[...], taken).astype(BF16)
            for m in range(2):
                for j in range(4):
                    at = (m * 4 + j) * 32
                    whole[m, rows_of(chunk, 32), j * 128 : (j + 1) * 128] = laid[at : at + 32]

        repeat(16, lay)

    def pick_pieces(target, table):
        def pick(i):
            rows = rows_of(i, 256)
            target[rows, :] = dot(choose[rows, :], table[...]).astype(BF16)

        repeat(4, pick)

    def send_pieces(slot, source, target):
        def send(i):
            pz, px, pc = peer_at(i + 1)
            peer = (pz * NX + px) * NC + pc
            pltpu.make_async_remote_copy(
                src_ref=source.at[rows_of(peer, PIECE)],
                dst_ref=target.at[rows_of(me, PIECE)],
                send_sem=send_sem.at[slot],
                recv_sem=recv_sem.at[slot],
                device_id=(pz, px, pc, y),
                device_id_type=MESH,
            ).start()

        repeat(PEERS - 1, send)

    sent_bytes = pl.ds(0, (PEERS - 1) * PIECE)

    spread_shard(0, shard_now, gather_now)
    loads[0].wait()
    pick_pieces(raw_send, features)
    send_pieces(3, raw_send, rim)
    rim[rows_of(me, PIECE), :] = raw_send[rows_of(me, PIECE), :]

    tile_of = lax.broadcasted_iota(jnp.int32, (8, 1024), 1) // 128
    tile_at = lax.broadcasted_iota(jnp.int32, (8, 1024), 0)
    wide_ids = dot(src_ref[...].astype(F32), (tile_of == tile_at).astype(F32))
    for i in range(8):
        src_wide[i * 8 : (i + 1) * 8, :] = jnp.broadcast_to(wide_ids[i : i + 1, :], (8, 1024))
    loads[1].wait()

    def densify(i):
        def column(b):
            target = jnp.full((8, 128), b, jnp.int32).astype(F32)
            total = jnp.zeros((128, 128), F32)
            for t in range(8):
                ids = src_wide[rows_of(i, 8), t * 128 : (t + 1) * 128]
                chosen = (ids == target).astype(F32)[0:1, :]
                total = total + tiles[i, t].astype(F32) * chosen
            dense[rows_of(i, 128), rows_of(b, 128)] = total.astype(BF16)

        repeat(16, column)

    repeat(3, densify)
    gather_y(0, gather_now)
    repeat(3, lambda i: densify(i + 3))
    gather_core(0, gather_now)
    repeat(2, lambda i: densify(i + 6))

    loads[2].wait()
    gather_end(0, gather_now, weights)

    def up(i):
        rows = rows_of(i, 256)
        upstream[rows, :] = dot_over_columns(out_grad[rows, :], weights[1]).astype(BF16)

    repeat(4, up)

    def rim_part(i):
        part = dot_over_rows(dense[:, rows_of(i + 4, 256)], upstream[...])
        grad_send[rows_of(i, 256), :] = part.astype(BF16)

    repeat(4, rim_part)
    send_pieces(4, grad_send, fresh_grads_hbm)
    own_grads = pltpu.make_async_copy(
        grad_send.at[rows_of(me, PIECE)], fresh_grads_hbm.at[rows_of(me, PIECE)], store_sem.at[0]
    )
    own_grads.start()

    loads[3].wait()
    loads[4].wait()
    def local_part(i):
        rows = rows_of(i, 256)
        row = lax.broadcasted_iota(jnp.int32, (256, NODES), 0) + i * 256
        placing = (row == wanted).astype(F32).astype(BF16)
        d_first[rows, :] = dot_over_rows(dense[:, rows], upstream[...]) + dot(
            placing, stale_grads[...]
        )

    repeat(4, local_part)

    def ahead(i):
        rows = rows_of(i, 256)
        p_local[rows, :] = dot(dense[rows, 0:NODES], features[...])
        p_stale[rows, :] = dot(dense[rows, NODES : 2 * NODES], stale_features[...])

    repeat(4, ahead)

    plane_bytes(3, rim.at[sent_bytes]).wait_recv()

    def first_layer(i):
        rows = rows_of(i, 256)
        p = (p_local[rows, :] + dot(dense[rows, NODES : 2 * NODES], rim[...])).astype(BF16)
        p_first[rows, :] = p
        zf = dot(p, weights[0])
        s = 1.0 / (1.0 + jnp.exp(-zf))
        hidden[rows, :] = (zf * s).astype(BF16)
        dz[rows, :] = (d_first[rows, :] * s * (1.0 + zf * (1.0 - s))).astype(BF16)

    repeat(4, first_layer)
    pick_pieces(feature_send, hidden)
    send_pieces(5, feature_send, fresh_features_hbm)
    own_features = pltpu.make_async_copy(
        feature_send.at[rows_of(me, PIECE)],
        fresh_features_hbm.at[rows_of(me, PIECE)],
        store_sem.at[1],
    )
    own_features.start()

    def second_layer(i):
        rows = rows_of(i, 256)
        p_second[rows, :] = (p_stale[rows, :] + dot(dense[rows, 0:NODES], hidden[...])).astype(BF16)

    repeat(4, second_layer)

    def grad_rows(i):
        chunk = 8
        first = dot_over_rows(p_first[:, rows_of(i, 256)], dz[...]).astype(BF16)
        second = dot_over_rows(p_second[:, rows_of(i, 256)], out_grad[...]).astype(BF16)
        for k in range(chunk):
            stacked = jnp.concatenate(
                [
                    g[k * 32 : (k + 1) * 32, j * 128 : (j + 1) * 128]
                    for g in (first, second)
                    for j in range(4)
                ],
                0,
            )
            blocks = dot(perm_back[...], stacked).astype(BF16)
            for a in range(8):
                grad_blocks[a // 4, a % 4, rows_of(i * chunk + k, 32), :] = blocks[
                    a * 32 : (a + 1) * 32
                ]

    repeat(2, grad_rows)

    pltpu.make_async_remote_copy(
        src_ref=grad_blocks.at[1 - c],
        dst_ref=from_core,
        send_sem=send_sem.at[6],
        recv_sem=recv_sem.at[6],
        device_id=(z, x, 1 - c, y),
        device_id_type=MESH,
    ).start()

    def last(i):
        rows = rows_of(i, 256)
        layer_out[rows, :] = dot(p_second[rows, :], weights[1]).astype(BF16)

    repeat(4, last)
    store_layer = pltpu.make_async_copy(layer_out, layer_out_hbm, store_sem.at[2])
    store_layer.start()

    plane_bytes(6, from_core).wait_recv()
    for k in range(NY):
        core_sum[k] = (grad_blocks[c, k].astype(F32) + from_core[k].astype(F32)).astype(BF16)
    for k in range(1, NY):
        pltpu.make_async_remote_copy(
            src_ref=core_sum.at[(y + k) % NY],
            dst_ref=from_y.at[k - 1],
            send_sem=send_sem.at[7],
            recv_sem=recv_sem.at[7],
            device_id=(z, x, c, (y + k) % NY),
            device_id_type=MESH,
        ).start()
    plane_bytes(7, from_y).wait_recv()
    y_sum[...] = (
        core_sum[y].astype(F32)
        + from_y[0].astype(F32)
        + from_y[1].astype(F32)
        + from_y[2].astype(F32)
    ).astype(BF16)
    from_plane[rows_of(plane, 16), :] = y_sum[rows_of(plane, 16), :]

    def send_shard(i):
        pz, px = plane_at(i + 1)
        pltpu.make_async_remote_copy(
            src_ref=y_sum.at[rows_of(pz * NX + px, 16)],
            dst_ref=from_plane.at[rows_of(plane, 16)],
            send_sem=send_sem.at[8],
            recv_sem=recv_sem.at[8],
            device_id=(pz, px, c, y),
            device_id_type=MESH,
        ).start()

    repeat(NZ * NX - 1, send_shard)
    plane_bytes(8, from_plane.at[pl.ds(0, 496)]).wait_recv()
    total = from_plane[0:16, :].astype(F32)
    for k in range(1, NZ * NX):
        total = total + from_plane[k * 16 : (k + 1) * 16, :].astype(F32)
    grads = total / TOTAL_NODES
    moment_new = decay_first * rows_f32[1] + (1.0 - decay_first) * grads
    second_new = decay_second * rows_f32[2] + (1.0 - decay_second) * grads * grads
    update = (
        moment_new
        / (1.0 - decay_first**STEP)
        / (jnp.sqrt(second_new / (1.0 - decay_second**STEP)) + epsilon)
    )
    master_next = rows_f32[0] - learn_rate * update
    rows_f32[3] = master_next
    shard_next[...] = master_next.astype(BF16)
    spread_shard(9, shard_next, gather_next)
    for m in range(2):
        for r in range(2):
            for j in range(4):
                s = m * 8 + r * 4 + j
                master_next_ref[m, r : r + 1, j * 128 : (j + 1) * 128] = rows_f32[3, s : s + 1, :]
    gather_y(9, gather_next)
    gather_core(9, gather_next)
    gather_end(9, gather_next, weights_next)
    store_weights = pltpu.make_async_copy(weights_next, weights_next_hbm, store_sem.at[3])
    store_weights.start()

    for slot, shard, gathered in ((0, gather_now, gather_now), (9, gather_next, gather_next)):
        plane_bytes(slot, gathered.at[0, 0, pl.ds(0, 496)]).wait_send()
        plane_bytes(slot + 1, gathered.at[0, pl.ds(0, 3)]).wait_send()
        plane_bytes(slot + 2, gathered.at[0]).wait_send()
    plane_bytes(6, from_core).wait_send()
    plane_bytes(7, from_y).wait_send()
    plane_bytes(8, from_plane.at[pl.ds(0, 496)]).wait_send()
    for slot, source in ((3, raw_send), (4, grad_send), (5, feature_send)):
        plane_bytes(slot, source.at[sent_bytes]).wait_send()
    plane_bytes(4, fresh_grads_hbm.at[sent_bytes]).wait_recv()
    plane_bytes(5, fresh_features_hbm.at[sent_bytes]).wait_recv()
    own_grads.wait()
    own_features.wait()
    store_layer.wait()
    store_weights.wait()


def per_device(
    features,
    tile_src,
    tile_val,
    send_sel,
    stale_features,
    stale_grads,
    out_grad,
    master,
    moment_first,
    moment_second,
):
    any_space = pl.BlockSpec(memory_space=pl.ANY)
    vmem = pl.BlockSpec(memory_space=pltpu.VMEM)
    nodes = pltpu.VMEM((NODES, F), BF16)
    nodes_f32 = pltpu.VMEM((NODES, F), F32)
    matrices = pltpu.VMEM((2, F, F), BF16)
    blocks = pltpu.VMEM((2, NY, 512, 128), BF16)
    half = pltpu.VMEM((NY, 512, 128), BF16)
    lines = pltpu.VMEM((512, 128), BF16)
    shard = pltpu.VMEM((16, 128), BF16)
    square = pltpu.VMEM((256, 256), BF16)
    rows = jax.ShapeDtypeStruct((NODES, F), BF16)
    return pl.pallas_call(
        kernel,
        out_shape=(
            rows,
            rows,
            rows,
            jax.ShapeDtypeStruct((2, 2, F), F32),
            jax.ShapeDtypeStruct((2, F, F), BF16),
        ),
        in_specs=[vmem, vmem, vmem, vmem, vmem] + [any_space] * 5,
        out_specs=(any_space, any_space, any_space, vmem, any_space),
        scratch_shapes=[
            nodes,
            nodes,
            pltpu.VMEM((8, 8, 128, 128), BF16),
            pltpu.VMEM((NODES, 2 * NODES), BF16),
            nodes,
            nodes,
            nodes,
            nodes,
            nodes,
            nodes,
            nodes,
            nodes_f32,
            nodes_f32,
            nodes_f32,
            nodes,
            nodes,
            nodes,
            nodes,
            nodes,
            matrices,
            matrices,
            blocks,
            blocks,
            blocks,
            half,
            half,
            pltpu.VMEM((NY - 1, 512, 128), BF16),
            lines,
            lines,
            shard,
            shard,
            pltpu.VMEM((4, 16, 128), F32),
            pltpu.VMEM((64, 1024), F32),
            pltpu.VMEM((NODES, 128), jnp.int32),
            pltpu.VMEM((NODES, NODES), BF16),
            square,
            square,
            pltpu.SemaphoreType.DMA((5,)),
            pltpu.SemaphoreType.DMA((4,)),
            pltpu.SemaphoreType.DMA((12,)),
            pltpu.SemaphoreType.DMA((12,)),
        ],
        compiler_params=pltpu.CompilerParams(
            collective_id=0, has_side_effects=True, vmem_limit_bytes=56 * 2**20
        ),
        cost_estimate=pl.CostEstimate(
            flops=12 * 2**30, bytes_accessed=12 * 2**20, transcendentals=2**20
        ),
    )(
        tile_src,
        send_sel,
        master,
        moment_first,
        moment_second,
        features,
        tile_val,
        stale_features,
        stale_grads,
        out_grad,
    )


def solution(mesh):
    torus = Mesh(mesh.devices.reshape(NZ, NX, NC, NY), DEVICES)
    nodes = P(DEVICES, None)
    parts = P(None, DEVICES, None)
    return jax.shard_map(
        per_device,
        mesh=torus,
        in_specs=(
            nodes,
            nodes,
            P(DEVICES, None, None, None),
            nodes,
            nodes,
            nodes,
            nodes,
            parts,
            parts,
            parts,
        ),
        out_specs=(nodes, nodes, nodes, parts, P()),
        check_vma=False,
    )
```

```python
import functools

import jax
import jax.numpy as jnp
from jax import lax
from jax.experimental import pallas as pl
from jax.experimental.pallas import tpu as pltpu
from jax.sharding import Mesh
from jax.sharding import PartitionSpec as P

STEP = 10
DEVICES = ("z", "x", "c", "y")
NZ, NX, NC, NY = 8, 4, 2, 4
PEERS = NZ * NX * NC
F = 512
NODES = 1024
PIECE = 16
TOTAL_NODES = 262144
MESH = pl.DeviceIdType.MESH
BF16 = jnp.bfloat16
F32 = jnp.float32

decay_first = 0.9
decay_second = 0.95
learn_rate = 0.01
epsilon = 1e-08


def dot(a, b):
    return jnp.dot(a, b, preferred_element_type=F32)


def dot_over_rows(a, b):
    return lax.dot_general(a, b, (((0,), (0,)), ((), ())), preferred_element_type=F32)


def dot_over_columns(a, b):
    return lax.dot_general(a, b, (((1,), (1,)), ((), ())), preferred_element_type=F32)


def rows_of(index, count):
    return pl.ds(pl.multiple_of(index * count, count), count)


def repeat(count, body):
    def step(i, carry):
        body(i)
        return carry

    lax.fori_loop(0, count, step, 0)


def kernel(
    src_ref,
    sel_row_ref,
    master_ref,
    first_ref,
    second_ref,
    features_hbm,
    tiles_hbm,
    stale_features_hbm,
    stale_grads_hbm,
    out_grad_hbm,
    layer_out_hbm,
    fresh_features_hbm,
    fresh_grads_hbm,
    master_next_ref,
    weights_next_hbm,
    features,
    rim,
    tiles,
    dense,
    dense_low,
    out_grad,
    stale_features,
    stale_grads,
    raw_send,
    feature_send,
    grad_send,
    upstream,
    p_local,
    p_stale,
    d_first,
    p_first,
    dz,
    hidden,
    p_second,
    layer_out,
    weights,
    weights_next,
    gather_now,
    gather_next,
    grad_blocks,
    from_core,
    core_sum,
    from_y,
    y_sum,
    from_plane,
    shard_now,
    shard_next,
    rows_f32,
    src_wide,
    want_down,
    choose,
    perm,
    perm_back,
    load_sem,
    store_sem,
    send_sem,
    recv_sem,
):
    z, x, c, y = (lax.axis_index(a) for a in DEVICES)
    plane = z * NX + x
    me = plane * NC + c

    loads = [
        pltpu.make_async_copy(s, d, load_sem.at[i])
        for i, (s, d) in enumerate(
            (
                (features_hbm, features),
                (tiles_hbm, tiles),
                (out_grad_hbm, out_grad),
                (stale_grads_hbm, stale_grads),
                (stale_features_hbm, stale_features),
            )
        )
    ]
    for load in loads:
        load.start()

    def peer_at(step):
        dz_, dx_, dc_ = step // 8, (step // 2) % 4, step % 2
        return ((z + dz_) % NZ, (x + dx_) % NX, (c + dc_) % NC)

    def plane_at(step):
        return ((z + step // 4) % NZ, (x + step % 4) % NX)

    barrier = pltpu.get_barrier_semaphore()

    def greet(i):
        pz, px, pc = peer_at(i + 1)
        pl.semaphore_signal(barrier, inc=1, device_id=(pz, px, pc, y), device_id_type=MESH)

    repeat(PEERS - 1, greet)
    for k in range(1, NY):
        pl.semaphore_signal(
            barrier, inc=1, device_id=(z, x, c, (y + k) % NY), device_id_type=MESH
        )

    def fill_rows(target, source):
        for m in range(2):
            for r in range(2):
                for j in range(4):
                    s = m * 8 + r * 4 + j
                    target[s : s + 1, :] = source[m, r : r + 1, j * 128 : (j + 1) * 128]

    fill_rows(rows_f32.at[0], master_ref)
    fill_rows(rows_f32.at[1], first_ref)
    fill_rows(rows_f32.at[2], second_ref)
    shard_now[...] = rows_f32[0].astype(BF16)

    def bits(o):
        m, j, p = o >> 7, (o >> 5) & 3, (o >> 4) & 1
        return (((o >> 3) & 1) << 7) | (((o >> 1) & 3) << 5) | (p << 4) | (m << 3) | ((o & 1) << 2) | j

    down = lax.broadcasted_iota(jnp.int32, (256, 256), 0)
    along = lax.broadcasted_iota(jnp.int32, (256, 256), 1)
    perm[...] = (bits(down) == along).astype(F32).astype(BF16)
    perm_back[...] = (bits(along) == down).astype(F32).astype(BF16)

    slot_of = lax.broadcasted_iota(jnp.int32, (PEERS, NODES), 1) // PIECE
    slot_at = lax.broadcasted_iota(jnp.int32, (PEERS, NODES), 0)
    widen = (slot_of == slot_at).astype(F32).astype(BF16)
    picks = jnp.broadcast_to(sel_row_ref[...].astype(F32), (16, PEERS)).astype(BF16)
    wide = dot(picks, widen)[0:1, :].astype(jnp.int32)
    lane = lax.broadcasted_iota(jnp.int32, (1, NODES), 1) % PIECE
    wanted = wide * PIECE + lane

    tall = dot_over_rows(widen, dot_over_rows(picks, jnp.full((16, 128), 0.0625, BF16)).astype(BF16))
    want_down[...] = tall.astype(jnp.int32) * PIECE + (
        lax.broadcasted_iota(jnp.int32, (NODES, 128), 0) % PIECE
    )

    def choose_rows(i):
        rows = rows_of(i, 256)
        for k in range(8):
            column = lax.broadcasted_iota(jnp.int32, (256, 128), 1) + k * 128
            chosen = (want_down[rows, :] == column).astype(F32).astype(BF16)
            choose[rows, k * 128 : (k + 1) * 128] = chosen

    repeat(4, choose_rows)

    pl.semaphore_wait(barrier, PEERS - 1 + NY - 1)

    def spread_shard(slot, shard, gathered):
        gathered[c, y, rows_of(plane, 16), :] = shard[...]

        def send(i):
            pz, px = plane_at(i + 1)
            pltpu.make_async_remote_copy(
                src_ref=shard,
                dst_ref=gathered.at[c, y, rows_of(plane, 16)],
                send_sem=send_sem.at[slot],
                recv_sem=recv_sem.at[slot],
                device_id=(pz, px, c, y),
                device_id_type=MESH,
            ).start()

        repeat(NZ * NX - 1, send)

    def plane_bytes(slot, ref):
        return pltpu.make_async_remote_copy(
            src_ref=ref,
            dst_ref=ref,
            send_sem=send_sem.at[slot],
            recv_sem=recv_sem.at[slot],
            device_id=(z, x, c, (y + 1) % NY),
            device_id_type=MESH,
        )

    def gather_y(slot, gathered):
        plane_bytes(slot, gathered.at[0, 0, pl.ds(0, 496)]).wait_recv()
        copies = [
            pltpu.make_async_remote_copy(
                src_ref=gathered.at[c, y],
                dst_ref=gathered.at[c, y],
                send_sem=send_sem.at[slot + 1],
                recv_sem=recv_sem.at[slot + 1],
                device_id=(z, x, c, (y + k) % NY),
                device_id_type=MESH,
            )
            for k in range(1, NY)
        ]
        for copy in copies:
            copy.start()

    def gather_core(slot, gathered):
        plane_bytes(slot + 1, gathered.at[0, pl.ds(0, 3)]).wait_recv()
        pltpu.make_async_remote_copy(
            src_ref=gathered.at[c],
            dst_ref=gathered.at[c],
            send_sem=send_sem.at[slot + 2],
            recv_sem=recv_sem.at[slot + 2],
            device_id=(z, x, 1 - c, y),
            device_id_type=MESH,
        ).start()

    def gather_end(slot, gathered, whole):
        plane_bytes(slot + 2, gathered.at[0]).wait_recv()

        def lay(chunk):
            taken = jnp.concatenate(
                [gathered[a // 4, a % 4, rows_of(chunk, 32), :] for a in range(8)], 0
            )
            laid = dot(perm[...], taken).astype(BF16)
            for m in range(2):
                for j in range(4):
                    at = (m * 4 + j) * 32
                    whole[m, rows_of(chunk, 32), j * 128 : (j + 1) * 128] = laid[at : at + 32]

        repeat(16, lay)

    def pick_pieces(target, table):
        def pick(i):
            rows = rows_of(i, 256)
            target[rows, :] = dot(choose[rows, :], table[...]).astype(BF16)

        repeat(4, pick)

    def send_pieces(slot, source, target):
        def send(i):
            pz, px, pc = peer_at(i + 1)
            peer = (pz * NX + px) * NC + pc
            pltpu.make_async_remote_copy(
                src_ref=source.at[rows_of(peer, PIECE)],
                dst_ref=target.at[rows_of(me, PIECE)],
                send_sem=send_sem.at[slot],
                recv_sem=recv_sem.at[slot],
                device_id=(pz, px, pc, y),
                device_id_type=MESH,
            ).start()

        repeat(PEERS - 1, send)

    sent_bytes = pl.ds(0, (PEERS - 1) * PIECE)

    spread_shard(0, shard_now, gather_now)
    loads[0].wait()
    pick_pieces(raw_send, features)
    send_pieces(3, raw_send, rim)
    rim[rows_of(me, PIECE), :] = raw_send[rows_of(me, PIECE), :]

    tile_of = lax.broadcasted_iota(jnp.int32, (8, 1024), 1) // 128
    tile_at = lax.broadcasted_iota(jnp.int32, (8, 1024), 0)
    wide_ids = dot(src_ref[...].astype(F32), (tile_of == tile_at).astype(F32))
    for i in range(8):
        src_wide[i * 8 : (i + 1) * 8, :] = jnp.broadcast_to(wide_ids[i : i + 1, :], (8, 1024))
    loads[1].wait()

    def densify(i):
        def column(b):
            target = jnp.full((8, 128), b, jnp.int32).astype(F32)
            total = jnp.zeros((128, 128), F32)
            for t in range(8):
                ids = src_wide[rows_of(i, 8), t * 128 : (t + 1) * 128]
                chosen = (ids == target).astype(F32)[0:1, :]
                total = total + tiles[i, t].astype(F32) * chosen
            high = total.astype(BF16)
            dense[rows_of(i, 128), rows_of(b, 128)] = high
            dense_low[rows_of(i, 128), rows_of(b, 128)] = (total - high.astype(F32)).astype(BF16)

        repeat(16, column)

    repeat(3, densify)
    gather_y(0, gather_now)
    repeat(3, lambda i: densify(i + 3))
    gather_core(0, gather_now)
    repeat(2, lambda i: densify(i + 6))

    loads[2].wait()
    gather_end(0, gather_now, weights)

    def tiles_on(rows, columns, table):
        return dot(dense[rows, columns], table) + dot(dense_low[rows, columns], table)

    def tiles_back(columns):
        return dot_over_rows(dense[:, columns], upstream[...]) + dot_over_rows(
            dense_low[:, columns], upstream[...]
        )

    def up(i):
        rows = rows_of(i, 256)
        upstream[rows, :] = dot_over_columns(out_grad[rows, :], weights[1]).astype(BF16)

    repeat(4, up)

    def rim_part(i):
        part = tiles_back(rows_of(i + 4, 256))
        grad_send[rows_of(i, 256), :] = part.astype(BF16)

    repeat(4, rim_part)
    send_pieces(4, grad_send, fresh_grads_hbm)
    own_grads = pltpu.make_async_copy(
        grad_send.at[rows_of(me, PIECE)], fresh_grads_hbm.at[rows_of(me, PIECE)], store_sem.at[0]
    )
    own_grads.start()

    loads[3].wait()
    loads[4].wait()
    def local_part(i):
        rows = rows_of(i, 256)
        row = lax.broadcasted_iota(jnp.int32, (256, NODES), 0) + i * 256
        placing = (row == wanted).astype(F32).astype(BF16)
        d_first[rows, :] = tiles_back(rows) + dot(placing, stale_grads[...])

    repeat(4, local_part)

    def ahead(i):
        rows = rows_of(i, 256)
        p_local[rows, :] = tiles_on(rows, slice(0, NODES), features[...])
        p_stale[rows, :] = tiles_on(rows, slice(NODES, 2 * NODES), stale_features[...])

    repeat(4, ahead)

    plane_bytes(3, rim.at[sent_bytes]).wait_recv()

    def first_layer(i):
        rows = rows_of(i, 256)
        p = (p_local[rows, :] + tiles_on(rows, slice(NODES, 2 * NODES), rim[...])).astype(BF16)
        p_first[rows, :] = p
        zf = dot(p, weights[0])
        s = 1.0 / (1.0 + jnp.exp(-zf))
        hidden[rows, :] = (zf * s).astype(BF16)
        dz[rows, :] = (d_first[rows, :] * s * (1.0 + zf * (1.0 - s))).astype(BF16)

    repeat(4, first_layer)
    pick_pieces(feature_send, hidden)
    send_pieces(5, feature_send, fresh_features_hbm)
    own_features = pltpu.make_async_copy(
        feature_send.at[rows_of(me, PIECE)],
        fresh_features_hbm.at[rows_of(me, PIECE)],
        store_sem.at[1],
    )
    own_features.start()

    def second_layer(i):
        rows = rows_of(i, 256)
        p_second[rows, :] = (p_stale[rows, :] + tiles_on(rows, slice(0, NODES), hidden[...])).astype(BF16)

    repeat(4, second_layer)

    def grad_rows(i):
        chunk = 8
        first = dot_over_rows(p_first[:, rows_of(i, 256)], dz[...]).astype(BF16)
        second = dot_over_rows(p_second[:, rows_of(i, 256)], out_grad[...]).astype(BF16)
        for k in range(chunk):
            stacked = jnp.concatenate(
                [
                    g[k * 32 : (k + 1) * 32, j * 128 : (j + 1) * 128]
                    for g in (first, second)
                    for j in range(4)
                ],
                0,
            )
            blocks = dot(perm_back[...], stacked).astype(BF16)
            for a in range(8):
                grad_blocks[a // 4, a % 4, rows_of(i * chunk + k, 32), :] = blocks[
                    a * 32 : (a + 1) * 32
                ]

    repeat(2, grad_rows)

    pltpu.make_async_remote_copy(
        src_ref=grad_blocks.at[1 - c],
        dst_ref=from_core,
        send_sem=send_sem.at[6],
        recv_sem=recv_sem.at[6],
        device_id=(z, x, 1 - c, y),
        device_id_type=MESH,
    ).start()

    def last(i):
        rows = rows_of(i, 256)
        layer_out[rows, :] = dot(p_second[rows, :], weights[1]).astype(BF16)

    repeat(4, last)
    store_layer = pltpu.make_async_copy(layer_out, layer_out_hbm, store_sem.at[2])
    store_layer.start()

    plane_bytes(6, from_core).wait_recv()
    for k in range(NY):
        core_sum[k] = (grad_blocks[c, k].astype(F32) + from_core[k].astype(F32)).astype(BF16)
    for k in range(1, NY):
        pltpu.make_async_remote_copy(
            src_ref=core_sum.at[(y + k) % NY],
            dst_ref=from_y.at[k - 1],
            send_sem=send_sem.at[7],
            recv_sem=recv_sem.at[7],
            device_id=(z, x, c, (y + k) % NY),
            device_id_type=MESH,
        ).start()
    plane_bytes(7, from_y).wait_recv()
    y_sum[...] = (
        core_sum[y].astype(F32)
        + from_y[0].astype(F32)
        + from_y[1].astype(F32)
        + from_y[2].astype(F32)
    ).astype(BF16)
    from_plane[rows_of(plane, 16), :] = y_sum[rows_of(plane, 16), :]

    def send_shard(i):
        pz, px = plane_at(i + 1)
        pltpu.make_async_remote_copy(
            src_ref=y_sum.at[rows_of(pz * NX + px, 16)],
            dst_ref=from_plane.at[rows_of(plane, 16)],
            send_sem=send_sem.at[8],
            recv_sem=recv_sem.at[8],
            device_id=(pz, px, c, y),
            device_id_type=MESH,
        ).start()

    repeat(NZ * NX - 1, send_shard)
    plane_bytes(8, from_plane.at[pl.ds(0, 496)]).wait_recv()
    total = from_plane[0:16, :].astype(F32)
    for k in range(1, NZ * NX):
        total = total + from_plane[k * 16 : (k + 1) * 16, :].astype(F32)
    grads = total / TOTAL_NODES
    moment_new = decay_first * rows_f32[1] + (1.0 - decay_first) * grads
    second_new = decay_second * rows_f32[2] + (1.0 - decay_second) * grads * grads
    update = (
        moment_new
        / (1.0 - decay_first**STEP)
        / (jnp.sqrt(second_new / (1.0 - decay_second**STEP)) + epsilon)
    )
    master_next = rows_f32[0] - learn_rate * update
    rows_f32[3] = master_next
    shard_next[...] = master_next.astype(BF16)
    spread_shard(9, shard_next, gather_next)
    for m in range(2):
        for r in range(2):
            for j in range(4):
                s = m * 8 + r * 4 + j
                master_next_ref[m, r : r + 1, j * 128 : (j + 1) * 128] = rows_f32[3, s : s + 1, :]
    gather_y(9, gather_next)
    gather_core(9, gather_next)
    gather_end(9, gather_next, weights_next)
    store_weights = pltpu.make_async_copy(weights_next, weights_next_hbm, store_sem.at[3])
    store_weights.start()

    for slot, shard, gathered in ((0, gather_now, gather_now), (9, gather_next, gather_next)):
        plane_bytes(slot, gathered.at[0, 0, pl.ds(0, 496)]).wait_send()
        plane_bytes(slot + 1, gathered.at[0, pl.ds(0, 3)]).wait_send()
        plane_bytes(slot + 2, gathered.at[0]).wait_send()
    plane_bytes(6, from_core).wait_send()
    plane_bytes(7, from_y).wait_send()
    plane_bytes(8, from_plane.at[pl.ds(0, 496)]).wait_send()
    for slot, source in ((3, raw_send), (4, grad_send), (5, feature_send)):
        plane_bytes(slot, source.at[sent_bytes]).wait_send()
    plane_bytes(4, fresh_grads_hbm.at[sent_bytes]).wait_recv()
    plane_bytes(5, fresh_features_hbm.at[sent_bytes]).wait_recv()
    own_grads.wait()
    own_features.wait()
    store_layer.wait()
    store_weights.wait()


def per_device(
    features,
    tile_src,
    tile_val,
    send_sel,
    stale_features,
    stale_grads,
    out_grad,
    master,
    moment_first,
    moment_second,
):
    any_space = pl.BlockSpec(memory_space=pl.ANY)
    vmem = pl.BlockSpec(memory_space=pltpu.VMEM)
    nodes = pltpu.VMEM((NODES, F), BF16)
    nodes_f32 = pltpu.VMEM((NODES, F), F32)
    matrices = pltpu.VMEM((2, F, F), BF16)
    blocks = pltpu.VMEM((2, NY, 512, 128), BF16)
    half = pltpu.VMEM((NY, 512, 128), BF16)
    lines = pltpu.VMEM((512, 128), BF16)
    shard = pltpu.VMEM((16, 128), BF16)
    square = pltpu.VMEM((256, 256), BF16)
    rows = jax.ShapeDtypeStruct((NODES, F), BF16)
    return pl.pallas_call(
        kernel,
        out_shape=(
            rows,
            rows,
            rows,
            jax.ShapeDtypeStruct((2, 2, F), F32),
            jax.ShapeDtypeStruct((2, F, F), BF16),
        ),
        in_specs=[vmem, vmem, vmem, vmem, vmem] + [any_space] * 5,
        out_specs=(any_space, any_space, any_space, vmem, any_space),
        scratch_shapes=[
            nodes,
            nodes,
            pltpu.VMEM((8, 8, 128, 128), BF16),
            pltpu.VMEM((NODES, 2 * NODES), BF16),
            pltpu.VMEM((NODES, 2 * NODES), BF16),
            nodes,
            nodes,
            nodes,
            nodes,
            nodes,
            nodes,
            nodes,
            nodes_f32,
            nodes_f32,
            nodes_f32,
            nodes,
            nodes,
            nodes,
            nodes,
            nodes,
            matrices,
            matrices,
            blocks,
            blocks,
            blocks,
            half,
            half,
            pltpu.VMEM((NY - 1, 512, 128), BF16),
            lines,
            lines,
            shard,
            shard,
            pltpu.VMEM((4, 16, 128), F32),
            pltpu.VMEM((64, 1024), F32),
            pltpu.VMEM((NODES, 128), jnp.int32),
            pltpu.VMEM((NODES, NODES), BF16),
            square,
            square,
            pltpu.SemaphoreType.DMA((5,)),
            pltpu.SemaphoreType.DMA((4,)),
            pltpu.SemaphoreType.DMA((12,)),
            pltpu.SemaphoreType.DMA((12,)),
        ],
        compiler_params=pltpu.CompilerParams(
            collective_id=0, has_side_effects=True, vmem_limit_bytes=56 * 2**20
        ),
        cost_estimate=pl.CostEstimate(
            flops=12 * 2**30, bytes_accessed=12 * 2**20, transcendentals=2**20
        ),
    )(
        tile_src,
        send_sel,
        master,
        moment_first,
        moment_second,
        features,
        tile_val,
        stale_features,
        stale_grads,
        out_grad,
    )


def solution(mesh):
    torus = Mesh(mesh.devices.reshape(NZ, NX, NC, NY), DEVICES)
    nodes = P(DEVICES, None)
    parts = P(None, DEVICES, None)
    return jax.shard_map(
        per_device,
        mesh=torus,
        in_specs=(
            nodes,
            nodes,
            P(DEVICES, None, None, None),
            nodes,
            nodes,
            nodes,
            nodes,
            parts,
            parts,
            parts,
        ),
        out_specs=(nodes, nodes, nodes, parts, P()),
        check_vma=False,
    )
```

```python
import functools

import jax
import jax.numpy as jnp
from jax import lax
from jax.experimental import pallas as pl
from jax.experimental.pallas import tpu as pltpu
from jax.sharding import Mesh
from jax.sharding import PartitionSpec as P

STEP = 10
DEVICES = ("z", "x", "c", "y")
NZ, NX, NC, NY = 8, 4, 2, 4
PEERS = NZ * NX * NC
F = 512
NODES = 1024
PIECE = 16
TOTAL_NODES = 262144
MESH = pl.DeviceIdType.MESH
BF16 = jnp.bfloat16
F32 = jnp.float32

decay_first = 0.9
decay_second = 0.95
learn_rate = 0.01
epsilon = 1e-08


def dot(a, b):
    return jnp.dot(a, b, preferred_element_type=F32)


def dot_over_rows(a, b):
    return lax.dot_general(a, b, (((0,), (0,)), ((), ())), preferred_element_type=F32)


def dot_over_columns(a, b):
    return lax.dot_general(a, b, (((1,), (1,)), ((), ())), preferred_element_type=F32)


def rows_of(index, count):
    return pl.ds(pl.multiple_of(index * count, count), count)


def repeat(count, body):
    def step(i, carry):
        body(i)
        return carry

    lax.fori_loop(0, count, step, 0)


def kernel(
    src_ref,
    sel_row_ref,
    master_ref,
    first_ref,
    second_ref,
    features_hbm,
    tiles_hbm,
    stale_features_hbm,
    stale_grads_hbm,
    out_grad_hbm,
    layer_out_hbm,
    fresh_features_hbm,
    fresh_grads_hbm,
    master_next_ref,
    weights_next_hbm,
    features,
    rim,
    tiles,
    dense,
    dense_low,
    out_grad,
    stale_features,
    stale_grads,
    raw_send,
    feature_send,
    grad_send,
    upstream,
    p_local,
    p_stale,
    d_first,
    p_first,
    dz,
    hidden,
    p_second,
    layer_out,
    weights,
    weights_next,
    gather_now,
    gather_next,
    grad_blocks,
    from_core,
    core_sum,
    from_across,
    across_sum,
    from_z,
    shard_now,
    shard_next,
    rows_f32,
    src_wide,
    want_down,
    choose,
    perm,
    perm_back,
    load_sem,
    store_sem,
    send_sem,
    recv_sem,
):
    z, x, c, y = (lax.axis_index(a) for a in DEVICES)
    column = x * NY + y
    me = (z * NX + x) * NC + c

    loads = [
        pltpu.make_async_copy(s, d, load_sem.at[i])
        for i, (s, d) in enumerate(
            (
                (features_hbm, features),
                (tiles_hbm, tiles),
                (out_grad_hbm, out_grad),
                (stale_grads_hbm, stale_grads),
                (stale_features_hbm, stale_features),
            )
        )
    ]
    for load in loads:
        load.start()

    def peer_at(step):
        turn, dx_, dc_ = step % 8, (step // 8) % 4, step // 32
        half = (turn + 1) // 2
        dz_ = half * (turn % 2) + (NZ - half) * (1 - turn % 2)
        return ((z + dz_) % NZ, (x + dx_) % NX, (c + dc_) % NC)

    def across(step):
        return ((x + step // NY) % NX, (y + step % NY) % NY)

    barrier = pltpu.get_barrier_semaphore()

    def greet(i):
        pz, px, pc = peer_at(i + 1)
        pl.semaphore_signal(barrier, inc=1, device_id=(pz, px, pc, y), device_id_type=MESH)

    repeat(PEERS - 1, greet)
    for step in range(1, NX * NY):
        if step % NY:
            px, py = across(step)
            pl.semaphore_signal(barrier, inc=1, device_id=(z, px, c, py), device_id_type=MESH)

    def fill_rows(target, source):
        for m in range(2):
            for r in range(2):
                for j in range(4):
                    s = m * 8 + r * 4 + j
                    target[s : s + 1, :] = source[m, r : r + 1, j * 128 : (j + 1) * 128]

    fill_rows(rows_f32.at[0], master_ref)
    fill_rows(rows_f32.at[1], first_ref)
    fill_rows(rows_f32.at[2], second_ref)
    shard_now[...] = rows_f32[0].astype(BF16)

    def bits(o):
        m, j, p = o >> 7, (o >> 5) & 3, (o >> 4) & 1
        return (((o >> 3) & 1) << 7) | (p << 6) | (((o >> 1) & 3) << 4) | (m << 3) | ((o & 1) << 2) | j

    down = lax.broadcasted_iota(jnp.int32, (256, 256), 0)
    along = lax.broadcasted_iota(jnp.int32, (256, 256), 1)
    perm[...] = (bits(down) == along).astype(F32).astype(BF16)
    perm_back[...] = (bits(along) == down).astype(F32).astype(BF16)

    slot_of = lax.broadcasted_iota(jnp.int32, (PEERS, NODES), 1) // PIECE
    slot_at = lax.broadcasted_iota(jnp.int32, (PEERS, NODES), 0)
    widen = (slot_of == slot_at).astype(F32).astype(BF16)
    picks = jnp.broadcast_to(sel_row_ref[...].astype(F32), (16, PEERS)).astype(BF16)
    wide = dot(picks, widen)[0:1, :].astype(jnp.int32)
    lane = lax.broadcasted_iota(jnp.int32, (1, NODES), 1) % PIECE
    wanted = wide * PIECE + lane

    tall = dot_over_rows(widen, dot_over_rows(picks, jnp.full((16, 128), 0.0625, BF16)).astype(BF16))
    want_down[...] = tall.astype(jnp.int32) * PIECE + (
        lax.broadcasted_iota(jnp.int32, (NODES, 128), 0) % PIECE
    )

    def choose_rows(i):
        rows = rows_of(i, 256)
        for k in range(8):
            column = lax.broadcasted_iota(jnp.int32, (256, 128), 1) + k * 128
            chosen = (want_down[rows, :] == column).astype(F32).astype(BF16)
            choose[rows, k * 128 : (k + 1) * 128] = chosen

    repeat(4, choose_rows)

    pl.semaphore_wait(barrier, PEERS - 1 + NX * (NY - 1))

    def spread_shard(slot, shard, gathered):
        gathered[c, column, rows_of(z, 16), :] = shard[...]
        for k in range(1, NZ):
            pltpu.make_async_remote_copy(
                src_ref=shard,
                dst_ref=gathered.at[c, column, rows_of(z, 16)],
                send_sem=send_sem.at[slot],
                recv_sem=recv_sem.at[slot],
                device_id=((z + k) % NZ, x, c, y),
                device_id_type=MESH,
            ).start()

    def total_of(slot, ref):
        return pltpu.make_async_remote_copy(
            src_ref=ref,
            dst_ref=ref,
            send_sem=send_sem.at[slot],
            recv_sem=recv_sem.at[slot],
            device_id=(z, x, c, (y + 1) % NY),
            device_id_type=MESH,
        )

    def gather_across(slot, gathered):
        total_of(slot, gathered.at[0, 0, pl.ds(0, 112)]).wait_recv()
        for step in range(1, NX * NY):
            px, py = across(step)
            pltpu.make_async_remote_copy(
                src_ref=gathered.at[c, column],
                dst_ref=gathered.at[c, column],
                send_sem=send_sem.at[slot + 1],
                recv_sem=recv_sem.at[slot + 1],
                device_id=(z, px, c, py),
                device_id_type=MESH,
            ).start()

    def gather_core(slot, gathered):
        total_of(slot + 1, gathered.at[0, pl.ds(0, 15)]).wait_recv()
        pltpu.make_async_remote_copy(
            src_ref=gathered.at[c],
            dst_ref=gathered.at[c],
            send_sem=send_sem.at[slot + 2],
            recv_sem=recv_sem.at[slot + 2],
            device_id=(z, x, 1 - c, y),
            device_id_type=MESH,
        ).start()

    def gather_end(slot, gathered, whole):
        total_of(slot + 2, gathered.at[0]).wait_recv()

        def lay(chunk):
            at_z, pair = rows_of(chunk // 2, 16), (chunk % 2) * 8
            taken = jnp.concatenate(
                [gathered[a // 8, pair + a % 8, at_z, :] for a in range(16)], 0
            )
            laid = dot(perm[...], taken).astype(BF16)
            for m in range(2):
                for j in range(4):
                    at = (m * 4 + j) * 32
                    whole[m, rows_of(chunk, 32), j * 128 : (j + 1) * 128] = laid[at : at + 32]

        repeat(16, lay)

    def pick_pieces(target, table):
        def pick(i):
            rows = rows_of(i, 256)
            target[rows, :] = dot(choose[rows, :], table[...]).astype(BF16)

        repeat(4, pick)

    def send_pieces(slot, source, target, begin, end):
        def send(i):
            pz, px, pc = peer_at(i + begin)
            peer = (pz * NX + px) * NC + pc
            pltpu.make_async_remote_copy(
                src_ref=source.at[rows_of(peer, PIECE)],
                dst_ref=target.at[rows_of(me, PIECE)],
                send_sem=send_sem.at[slot],
                recv_sem=recv_sem.at[slot],
                device_id=(pz, px, pc, y),
                device_id_type=MESH,
            ).start()

        repeat(end - begin, send)

    sent_bytes = pl.ds(0, (PEERS - 1) * PIECE)

    spread_shard(0, shard_now, gather_now)
    loads[0].wait()
    pick_pieces(raw_send, features)
    send_pieces(3, raw_send, rim, 1, 16)
    rim[rows_of(me, PIECE), :] = raw_send[rows_of(me, PIECE), :]

    tile_of = lax.broadcasted_iota(jnp.int32, (8, 1024), 1) // 128
    tile_at = lax.broadcasted_iota(jnp.int32, (8, 1024), 0)
    wide_ids = dot(src_ref[...].astype(F32), (tile_of == tile_at).astype(F32))
    for i in range(8):
        src_wide[i * 8 : (i + 1) * 8, :] = jnp.broadcast_to(wide_ids[i : i + 1, :], (8, 1024))
    loads[1].wait()

    def densify(i):
        def column(b):
            target = jnp.full((8, 128), b, jnp.int32).astype(F32)
            total = jnp.zeros((128, 128), F32)
            for t in range(8):
                ids = src_wide[rows_of(i, 8), t * 128 : (t + 1) * 128]
                chosen = (ids == target).astype(F32)[0:1, :]
                total = total + tiles[i, t].astype(F32) * chosen
            high = total.astype(BF16)
            dense[rows_of(i, 128), rows_of(b, 128)] = high
            dense_low[rows_of(i, 128), rows_of(b, 128)] = (total - high.astype(F32)).astype(BF16)

        repeat(16, column)

    repeat(1, densify)
    gather_across(0, gather_now)
    send_pieces(3, raw_send, rim, 16, 40)
    repeat(3, lambda i: densify(i + 1))
    gather_core(0, gather_now)
    send_pieces(3, raw_send, rim, 40, 64)
    repeat(4, lambda i: densify(i + 4))

    loads[2].wait()
    gather_end(0, gather_now, weights)

    def tiles_on(rows, columns, table):
        return dot(dense[rows, columns], table) + dot(dense_low[rows, columns], table)

    def tiles_back(columns):
        return dot_over_rows(dense[:, columns], upstream[...]) + dot_over_rows(
            dense_low[:, columns], upstream[...]
        )

    def up(i):
        rows = rows_of(i, 256)
        upstream[rows, :] = dot_over_columns(out_grad[rows, :], weights[1]).astype(BF16)

    repeat(4, up)

    def rim_part(i):
        part = tiles_back(rows_of(i + 4, 256))
        grad_send[rows_of(i, 256), :] = part.astype(BF16)

    repeat(4, rim_part)
    send_pieces(4, grad_send, fresh_grads_hbm, 1, 32)
    own_grads = pltpu.make_async_copy(
        grad_send.at[rows_of(me, PIECE)], fresh_grads_hbm.at[rows_of(me, PIECE)], store_sem.at[0]
    )
    own_grads.start()

    loads[3].wait()
    loads[4].wait()
    def local_part(i):
        rows = rows_of(i, 256)
        row = lax.broadcasted_iota(jnp.int32, (256, NODES), 0) + i * 256
        placing = (row == wanted).astype(F32).astype(BF16)
        d_first[rows, :] = tiles_back(rows) + dot(placing, stale_grads[...])

    repeat(4, local_part)

    def ahead(i):
        rows = rows_of(i, 256)
        p_local[rows, :] = tiles_on(rows, slice(0, NODES), features[...])
        p_stale[rows, :] = tiles_on(rows, slice(NODES, 2 * NODES), stale_features[...])

    repeat(4, ahead)

    total_of(3, rim.at[sent_bytes]).wait_recv()

    def first_layer(i):
        rows = rows_of(i, 256)
        p = (p_local[rows, :] + tiles_on(rows, slice(NODES, 2 * NODES), rim[...])).astype(BF16)
        p_first[rows, :] = p
        zf = dot(p, weights[0])
        s = 1.0 / (1.0 + jnp.exp(-zf))
        hidden[rows, :] = (zf * s).astype(BF16)
        dz[rows, :] = (d_first[rows, :] * s * (1.0 + zf * (1.0 - s))).astype(BF16)

    repeat(4, first_layer)
    pick_pieces(feature_send, hidden)
    own_features = pltpu.make_async_copy(
        feature_send.at[rows_of(me, PIECE)],
        fresh_features_hbm.at[rows_of(me, PIECE)],
        store_sem.at[1],
    )
    own_features.start()

    def second_layer(i):
        rows = rows_of(i, 256)
        p_second[rows, :] = (p_stale[rows, :] + tiles_on(rows, slice(0, NODES), hidden[...])).astype(BF16)

    repeat(4, second_layer)

    def grad_rows(i):
        chunk = 8
        first = dot_over_rows(p_first[:, rows_of(i, 256)], dz[...]).astype(BF16)
        second = dot_over_rows(p_second[:, rows_of(i, 256)], out_grad[...]).astype(BF16)
        for k in range(chunk):
            stacked = jnp.concatenate(
                [
                    g[k * 32 : (k + 1) * 32, j * 128 : (j + 1) * 128]
                    for g in (first, second)
                    for j in range(4)
                ],
                0,
            )
            blocks = dot(perm_back[...], stacked).astype(BF16)
            at_z, pair = rows_of(i * 4 + k // 2, 16), (k % 2) * 8
            for a in range(16):
                grad_blocks[a // 8, pair + a % 8, at_z, :] = blocks[a * 16 : (a + 1) * 16]

    repeat(2, grad_rows)

    pltpu.make_async_remote_copy(
        src_ref=grad_blocks.at[1 - c],
        dst_ref=from_core,
        send_sem=send_sem.at[6],
        recv_sem=recv_sem.at[6],
        device_id=(z, x, 1 - c, y),
        device_id_type=MESH,
    ).start()

    send_pieces(4, grad_send, fresh_grads_hbm, 32, 48)

    def last(i):
        rows = rows_of(i, 256)
        layer_out[rows, :] = dot(p_second[rows, :], weights[1]).astype(BF16)

    repeat(4, last)
    store_layer = pltpu.make_async_copy(layer_out, layer_out_hbm, store_sem.at[2])
    store_layer.start()

    total_of(6, from_core).wait_recv()

    def add_core(k):
        core_sum[k] = (grad_blocks[c, k].astype(F32) + from_core[k].astype(F32)).astype(BF16)

    repeat(NX * NY, add_core)
    for step in range(1, NX * NY):
        px, py = across(step)
        pltpu.make_async_remote_copy(
            src_ref=core_sum.at[px * NY + py],
            dst_ref=from_across.at[step - 1],
            send_sem=send_sem.at[7],
            recv_sem=recv_sem.at[7],
            device_id=(z, px, c, py),
            device_id_type=MESH,
        ).start()
    send_pieces(4, grad_send, fresh_grads_hbm, 48, 64)
    total_of(7, from_across).wait_recv()
    across_total = core_sum[column].astype(F32)
    for k in range(NX * NY - 1):
        across_total = across_total + from_across[k].astype(F32)
    across_sum[...] = across_total.astype(BF16)
    from_z[rows_of(z, 16), :] = across_sum[rows_of(z, 16), :]
    for k in range(1, NZ):
        pz = (z + k) % NZ
        pltpu.make_async_remote_copy(
            src_ref=across_sum.at[rows_of(pz, 16)],
            dst_ref=from_z.at[rows_of(z, 16)],
            send_sem=send_sem.at[8],
            recv_sem=recv_sem.at[8],
            device_id=(pz, x, c, y),
            device_id_type=MESH,
        ).start()
    send_pieces(5, feature_send, fresh_features_hbm, 1, 16)
    total_of(8, from_z.at[pl.ds(0, 112)]).wait_recv()
    total = from_z[0:16, :].astype(F32)
    for k in range(1, NZ):
        total = total + from_z[k * 16 : (k + 1) * 16, :].astype(F32)
    grads = total / TOTAL_NODES
    moment_new = decay_first * rows_f32[1] + (1.0 - decay_first) * grads
    second_new = decay_second * rows_f32[2] + (1.0 - decay_second) * grads * grads
    update = (
        moment_new
        / (1.0 - decay_first**STEP)
        / (jnp.sqrt(second_new / (1.0 - decay_second**STEP)) + epsilon)
    )
    master_next = rows_f32[0] - learn_rate * update
    rows_f32[3] = master_next
    shard_next[...] = master_next.astype(BF16)
    spread_shard(9, shard_next, gather_next)
    send_pieces(5, feature_send, fresh_features_hbm, 16, 28)
    for m in range(2):
        for r in range(2):
            for j in range(4):
                s = m * 8 + r * 4 + j
                master_next_ref[m, r : r + 1, j * 128 : (j + 1) * 128] = rows_f32[3, s : s + 1, :]
    gather_across(9, gather_next)
    send_pieces(5, feature_send, fresh_features_hbm, 28, 44)
    gather_core(9, gather_next)
    send_pieces(5, feature_send, fresh_features_hbm, 44, 64)
    gather_end(9, gather_next, weights_next)
    store_weights = pltpu.make_async_copy(weights_next, weights_next_hbm, store_sem.at[3])
    store_weights.start()

    for slot, gathered in ((0, gather_now), (9, gather_next)):
        total_of(slot, gathered.at[0, 0, pl.ds(0, 112)]).wait_send()
        total_of(slot + 1, gathered.at[0, pl.ds(0, 15)]).wait_send()
        total_of(slot + 2, gathered.at[0]).wait_send()
    total_of(6, from_core).wait_send()
    total_of(7, from_across).wait_send()
    total_of(8, from_z.at[pl.ds(0, 112)]).wait_send()
    for slot, source in ((3, raw_send), (4, grad_send), (5, feature_send)):
        total_of(slot, source.at[sent_bytes]).wait_send()
    total_of(4, fresh_grads_hbm.at[sent_bytes]).wait_recv()
    total_of(5, fresh_features_hbm.at[sent_bytes]).wait_recv()
    own_grads.wait()
    own_features.wait()
    store_layer.wait()
    store_weights.wait()


def deliver(*refs):
    sources, targets, sem = refs[:5], refs[5:10], refs[10]
    copies = [
        pltpu.make_async_copy(s, t, sem.at[i]) for i, (s, t) in enumerate(zip(sources, targets))
    ]
    for copy in copies:
        copy.start()
    for copy in copies:
        copy.wait()


def per_device(
    features,
    tile_src,
    tile_val,
    send_sel,
    stale_features,
    stale_grads,
    out_grad,
    master,
    moment_first,
    moment_second,
):
    any_space = pl.BlockSpec(memory_space=pl.ANY)
    vmem = pl.BlockSpec(memory_space=pltpu.VMEM)
    nodes = pltpu.VMEM((NODES, F), BF16)
    nodes_f32 = pltpu.VMEM((NODES, F), F32)
    matrices = pltpu.VMEM((2, F, F), BF16)
    blocks = pltpu.VMEM((2, NX * NY, 128, 128), BF16)
    half = pltpu.VMEM((NX * NY, 128, 128), BF16)
    lines = pltpu.VMEM((128, 128), BF16)
    shard = pltpu.VMEM((16, 128), BF16)
    square = pltpu.VMEM((256, 256), BF16)
    rows = jax.ShapeDtypeStruct((NODES, F), BF16)
    shapes = (
        rows,
        rows,
        rows,
        jax.ShapeDtypeStruct((2, 2, F), F32),
        jax.ShapeDtypeStruct((2, F, F), BF16),
    )
    made = pl.pallas_call(
        kernel,
        out_shape=shapes,
        in_specs=[vmem, vmem, vmem, vmem, vmem] + [any_space] * 5,
        out_specs=(any_space, any_space, any_space, vmem, any_space),
        scratch_shapes=[
            nodes,
            nodes,
            pltpu.VMEM((8, 8, 128, 128), BF16),
            pltpu.VMEM((NODES, 2 * NODES), BF16),
            pltpu.VMEM((NODES, 2 * NODES), BF16),
            nodes,
            nodes,
            nodes,
            nodes,
            nodes,
            nodes,
            nodes,
            nodes_f32,
            nodes_f32,
            nodes_f32,
            nodes,
            nodes,
            nodes,
            nodes,
            nodes,
            matrices,
            matrices,
            blocks,
            blocks,
            blocks,
            half,
            half,
            pltpu.VMEM((NX * NY - 1, 128, 128), BF16),
            lines,
            lines,
            shard,
            shard,
            pltpu.VMEM((4, 16, 128), F32),
            pltpu.VMEM((64, 1024), F32),
            pltpu.VMEM((NODES, 128), jnp.int32),
            pltpu.VMEM((NODES, NODES), BF16),
            square,
            square,
            pltpu.SemaphoreType.DMA((5,)),
            pltpu.SemaphoreType.DMA((4,)),
            pltpu.SemaphoreType.DMA((12,)),
            pltpu.SemaphoreType.DMA((12,)),
        ],
        compiler_params=pltpu.CompilerParams(
            collective_id=0, has_side_effects=True, vmem_limit_bytes=56 * 2**20
        ),
        cost_estimate=pl.CostEstimate(
            flops=12 * 2**30, bytes_accessed=12 * 2**20, transcendentals=2**20
        ),
    )(
        tile_src,
        send_sel,
        master,
        moment_first,
        moment_second,
        features,
        tile_val,
        stale_features,
        stale_grads,
        out_grad,
    )
    return pl.pallas_call(
        deliver,
        out_shape=shapes,
        in_specs=[any_space] * 5,
        out_specs=(any_space,) * 5,
        scratch_shapes=[pltpu.SemaphoreType.DMA((5,))],
    )(*made)


def solution(mesh):
    torus = Mesh(mesh.devices.reshape(NZ, NX, NC, NY), DEVICES)
    nodes = P(DEVICES, None)
    parts = P(None, DEVICES, None)
    return jax.shard_map(
        per_device,
        mesh=torus,
        in_specs=(
            nodes,
            nodes,
            P(DEVICES, None, None, None),
            nodes,
            nodes,
            nodes,
            nodes,
            parts,
            parts,
            parts,
        ),
        out_specs=(nodes, nodes, nodes, parts, P()),
        check_vma=False,
    )
```

```python
import functools

import jax
import jax.numpy as jnp
from jax import lax
from jax.experimental import pallas as pl
from jax.experimental.pallas import tpu as pltpu
from jax.sharding import Mesh
from jax.sharding import PartitionSpec as P

STEP = 10
DEVICES = ("z", "x", "c", "y")
NZ, NX, NC, NY = 8, 4, 2, 4
PEERS = NZ * NX * NC
F = 512
NODES = 1024
PIECE = 16
TOTAL_NODES = 262144
MESH = pl.DeviceIdType.MESH
BF16 = jnp.bfloat16
F32 = jnp.float32

decay_first = 0.9
decay_second = 0.95
learn_rate = 0.01
epsilon = 1e-08


def dot(a, b):
    return jnp.dot(a, b, preferred_element_type=F32)


def dot_over_rows(a, b):
    return lax.dot_general(a, b, (((0,), (0,)), ((), ())), preferred_element_type=F32)


def dot_over_columns(a, b):
    return lax.dot_general(a, b, (((1,), (1,)), ((), ())), preferred_element_type=F32)


def rows_of(index, count):
    return pl.ds(pl.multiple_of(index * count, count), count)


def repeat(count, body):
    def step(i, carry):
        body(i)
        return carry

    lax.fori_loop(0, count, step, 0)


def kernel(
    src_ref,
    sel_row_ref,
    master_ref,
    first_ref,
    second_ref,
    features_hbm,
    tiles_hbm,
    stale_features_hbm,
    stale_grads_hbm,
    out_grad_hbm,
    layer_out_hbm,
    fresh_features_hbm,
    fresh_grads_hbm,
    master_next_ref,
    weights_next_hbm,
    features,
    rim,
    tiles,
    dense,
    dense_low,
    out_grad,
    stale_features,
    stale_grads,
    raw_send,
    feature_send,
    grad_send,
    upstream,
    p_local,
    p_stale,
    d_first,
    p_first,
    dz,
    hidden,
    p_second,
    layer_out,
    weights,
    weights_next,
    gather_now,
    gather_next,
    grad_blocks,
    from_core,
    core_sum,
    from_across,
    across_sum,
    from_z,
    shard_now,
    shard_next,
    rows_f32,
    src_wide,
    want_down,
    choose,
    perm,
    perm_back,
    load_sem,
    store_sem,
    send_sem,
    recv_sem,
):
    z, x, c, y = (lax.axis_index(a) for a in DEVICES)
    column = x * NY + y
    me = (z * NX + x) * NC + c

    loads = [
        pltpu.make_async_copy(s, d, load_sem.at[i])
        for i, (s, d) in enumerate(
            (
                (features_hbm, features),
                (tiles_hbm, tiles),
                (out_grad_hbm, out_grad),
                (stale_grads_hbm, stale_grads),
                (stale_features_hbm, stale_features),
            )
        )
    ]
    for load in loads:
        load.start()

    def peer_at(step):
        turn, dx_, dc_ = step % 8, (step // 8) % 4, step // 32
        half = (turn + 1) // 2
        dz_ = half * (turn % 2) + (NZ - half) * (1 - turn % 2)
        return ((z + dz_) % NZ, (x + dx_) % NX, (c + dc_) % NC)

    def across(step):
        return ((x + step // NY) % NX, (y + step % NY) % NY)

    barrier = pltpu.get_barrier_semaphore()

    def greet(i):
        pz, px, pc = peer_at(i + 1)
        pl.semaphore_signal(barrier, inc=1, device_id=(pz, px, pc, y), device_id_type=MESH)

    repeat(PEERS - 1, greet)
    for step in range(1, NX * NY):
        if step % NY:
            px, py = across(step)
            pl.semaphore_signal(barrier, inc=1, device_id=(z, px, c, py), device_id_type=MESH)

    def fill_rows(target, source):
        for m in range(2):
            for r in range(2):
                for j in range(4):
                    s = m * 8 + r * 4 + j
                    target[s : s + 1, :] = source[m, r : r + 1, j * 128 : (j + 1) * 128]

    fill_rows(rows_f32.at[0], master_ref)
    fill_rows(rows_f32.at[1], first_ref)
    fill_rows(rows_f32.at[2], second_ref)
    shard_now[...] = rows_f32[0].astype(BF16)

    def bits(o):
        m, j, p = o >> 7, (o >> 5) & 3, (o >> 4) & 1
        return (((o >> 3) & 1) << 7) | (p << 6) | (((o >> 1) & 3) << 4) | (m << 3) | ((o & 1) << 2) | j

    down = lax.broadcasted_iota(jnp.int32, (256, 256), 0)
    along = lax.broadcasted_iota(jnp.int32, (256, 256), 1)
    perm[...] = (bits(down) == along).astype(F32).astype(BF16)
    perm_back[...] = (bits(along) == down).astype(F32).astype(BF16)

    slot_of = lax.broadcasted_iota(jnp.int32, (PEERS, NODES), 1) // PIECE
    slot_at = lax.broadcasted_iota(jnp.int32, (PEERS, NODES), 0)
    widen = (slot_of == slot_at).astype(F32).astype(BF16)
    picks = jnp.broadcast_to(sel_row_ref[...].astype(F32), (16, PEERS)).astype(BF16)
    wide = dot(picks, widen)[0:1, :].astype(jnp.int32)
    lane = lax.broadcasted_iota(jnp.int32, (1, NODES), 1) % PIECE
    wanted = wide * PIECE + lane

    tall = dot_over_rows(widen, dot_over_rows(picks, jnp.full((16, 128), 0.0625, BF16)).astype(BF16))
    want_down[...] = tall.astype(jnp.int32) * PIECE + (
        lax.broadcasted_iota(jnp.int32, (NODES, 128), 0) % PIECE
    )

    def choose_rows(i):
        rows = rows_of(i, 256)
        for k in range(8):
            column = lax.broadcasted_iota(jnp.int32, (256, 128), 1) + k * 128
            chosen = (want_down[rows, :] == column).astype(F32).astype(BF16)
            choose[rows, k * 128 : (k + 1) * 128] = chosen

    repeat(4, choose_rows)

    pl.semaphore_wait(barrier, PEERS - 1 + NX * (NY - 1))

    def spread_shard(slot, shard, gathered):
        gathered[c, column, rows_of(z, 16), :] = shard[...]
        for k in range(1, NZ):
            pltpu.make_async_remote_copy(
                src_ref=shard,
                dst_ref=gathered.at[c, column, rows_of(z, 16)],
                send_sem=send_sem.at[slot],
                recv_sem=recv_sem.at[slot],
                device_id=((z + k) % NZ, x, c, y),
                device_id_type=MESH,
            ).start()

    def total_of(slot, ref):
        return pltpu.make_async_remote_copy(
            src_ref=ref,
            dst_ref=ref,
            send_sem=send_sem.at[slot],
            recv_sem=recv_sem.at[slot],
            device_id=(z, x, c, (y + 1) % NY),
            device_id_type=MESH,
        )

    def gather_across(slot, gathered):
        total_of(slot, gathered.at[0, 0, pl.ds(0, 112)]).wait_recv()
        for step in range(1, NX * NY):
            px, py = across(step)
            pltpu.make_async_remote_copy(
                src_ref=gathered.at[c, column],
                dst_ref=gathered.at[c, column],
                send_sem=send_sem.at[slot + 1],
                recv_sem=recv_sem.at[slot + 1],
                device_id=(z, px, c, py),
                device_id_type=MESH,
            ).start()

    def gather_core(slot, gathered):
        total_of(slot + 1, gathered.at[0, pl.ds(0, 15)]).wait_recv()
        pltpu.make_async_remote_copy(
            src_ref=gathered.at[c],
            dst_ref=gathered.at[c],
            send_sem=send_sem.at[slot + 2],
            recv_sem=recv_sem.at[slot + 2],
            device_id=(z, x, 1 - c, y),
            device_id_type=MESH,
        ).start()

    def gather_end(slot, gathered, whole):
        total_of(slot + 2, gathered.at[0]).wait_recv()

        def lay(group):
            taken = jnp.concatenate(
                [
                    jnp.concatenate(
                        [
                            gathered[a // 8, (k % 2) * 8 + a % 8, rows_of(group * 2 + k // 2, 16), :]
                            for a in range(16)
                        ],
                        0,
                    )
                    for k in range(4)
                ],
                1,
            )
            laid = dot(perm[...], taken).astype(BF16)
            for k in range(4):
                rows = rows_of(group * 4 + k, 32)
                for m in range(2):
                    for j in range(4):
                        at = (m * 4 + j) * 32
                        whole[m, rows, j * 128 : (j + 1) * 128] = laid[
                            at : at + 32, k * 128 : (k + 1) * 128
                        ]

        repeat(4, lay)

    def pick_pieces(target, table):
        def pick(i):
            rows = rows_of(i, 256)
            target[rows, :] = dot(choose[rows, :], table[...]).astype(BF16)

        repeat(4, pick)

    def send_pieces(slot, source, target, begin, end):
        def send(i):
            pz, px, pc = peer_at(i + begin)
            peer = (pz * NX + px) * NC + pc
            pltpu.make_async_remote_copy(
                src_ref=source.at[rows_of(peer, PIECE)],
                dst_ref=target.at[rows_of(me, PIECE)],
                send_sem=send_sem.at[slot],
                recv_sem=recv_sem.at[slot],
                device_id=(pz, px, pc, y),
                device_id_type=MESH,
            ).start()

        repeat(end - begin, send)

    sent_bytes = pl.ds(0, (PEERS - 1) * PIECE)

    spread_shard(0, shard_now, gather_now)
    loads[0].wait()
    pick_pieces(raw_send, features)
    rim[rows_of(me, PIECE), :] = raw_send[rows_of(me, PIECE), :]

    tile_of = lax.broadcasted_iota(jnp.int32, (8, 1024), 1) // 128
    tile_at = lax.broadcasted_iota(jnp.int32, (8, 1024), 0)
    wide_ids = dot(src_ref[...].astype(F32), (tile_of == tile_at).astype(F32))
    for i in range(8):
        src_wide[i * 8 : (i + 1) * 8, :] = jnp.broadcast_to(wide_ids[i : i + 1, :], (8, 1024))
    loads[1].wait()

    def densify(i):
        def column(b):
            target = jnp.full((8, 128), b, jnp.int32).astype(F32)
            total = jnp.zeros((128, 128), F32)
            for t in range(8):
                ids = src_wide[rows_of(i, 8), t * 128 : (t + 1) * 128]
                chosen = (ids == target).astype(F32)[0:1, :]
                total = total + tiles[i, t].astype(F32) * chosen
            high = total.astype(BF16)
            dense[rows_of(i, 128), rows_of(b, 128)] = high
            dense_low[rows_of(i, 128), rows_of(b, 128)] = (total - high.astype(F32)).astype(BF16)

        repeat(16, column)

    repeat(1, densify)
    gather_across(0, gather_now)
    send_pieces(3, raw_send, rim, 1, 32)
    repeat(3, lambda i: densify(i + 1))
    gather_core(0, gather_now)
    send_pieces(3, raw_send, rim, 32, 64)
    repeat(4, lambda i: densify(i + 4))

    loads[2].wait()
    loads[4].wait()

    def tiles_on(rows, columns, table):
        return dot(dense[rows, columns], table) + dot(dense_low[rows, columns], table)

    def ahead(i):
        rows = rows_of(i, 256)
        p_local[rows, :] = tiles_on(rows, slice(0, NODES), features[...])
        p_stale[rows, :] = tiles_on(rows, slice(NODES, 2 * NODES), stale_features[...])

    repeat(4, ahead)

    gather_end(0, gather_now, weights)

    def tiles_back(columns):
        return dot(upstream[...], dense[:, columns]) + dot(upstream[...], dense_low[:, columns])

    def up(i):
        rows = rows_of(i, 256)
        upstream[:, rows] = dot_over_columns(weights[1], out_grad[rows, :]).astype(BF16)

    repeat(4, up)

    def rim_part(i):
        part = tiles_back(rows_of(i + 4, 256))
        grad_send[rows_of(i, 256), :] = part.astype(BF16).T

    repeat(4, rim_part)
    send_pieces(4, grad_send, fresh_grads_hbm, 1, 48)
    own_grads = pltpu.make_async_copy(
        grad_send.at[rows_of(me, PIECE)], fresh_grads_hbm.at[rows_of(me, PIECE)], store_sem.at[0]
    )
    own_grads.start()

    loads[3].wait()
    def local_part(i):
        rows = rows_of(i, 256)
        row = lax.broadcasted_iota(jnp.int32, (256, NODES), 0) + i * 256
        placing = (row == wanted).astype(F32).astype(BF16)
        d_first[rows, :] = tiles_back(rows).T + dot(placing, stale_grads[...])

    repeat(4, local_part)


    total_of(3, rim.at[sent_bytes]).wait_recv()

    def first_layer(i):
        rows = rows_of(i, 256)
        p = (p_local[rows, :] + tiles_on(rows, slice(NODES, 2 * NODES), rim[...])).astype(BF16)
        p_first[rows, :] = p
        zf = dot(p, weights[0])
        s = 1.0 / (1.0 + jnp.exp(-zf))
        hidden[rows, :] = (zf * s).astype(BF16)
        dz[rows, :] = (d_first[rows, :] * s * (1.0 + zf * (1.0 - s))).astype(BF16)

    repeat(4, first_layer)
    pick_pieces(feature_send, hidden)
    send_pieces(4, grad_send, fresh_grads_hbm, 48, 64)
    own_features = pltpu.make_async_copy(
        feature_send.at[rows_of(me, PIECE)],
        fresh_features_hbm.at[rows_of(me, PIECE)],
        store_sem.at[1],
    )
    own_features.start()

    def second_layer(i):
        rows = rows_of(i, 256)
        p_second[rows, :] = (p_stale[rows, :] + tiles_on(rows, slice(0, NODES), hidden[...])).astype(BF16)

    repeat(4, second_layer)

    def grad_rows(i):
        chunk = 8
        first = dot_over_rows(p_first[:, rows_of(i, 256)], dz[...]).astype(BF16)
        second = dot_over_rows(p_second[:, rows_of(i, 256)], out_grad[...]).astype(BF16)
        for k in range(chunk):
            stacked = jnp.concatenate(
                [
                    g[k * 32 : (k + 1) * 32, j * 128 : (j + 1) * 128]
                    for g in (first, second)
                    for j in range(4)
                ],
                0,
            )
            blocks = dot(perm_back[...], stacked).astype(BF16)
            at_z, pair = rows_of(i * 4 + k // 2, 16), (k % 2) * 8
            for a in range(16):
                grad_blocks[a // 8, pair + a % 8, at_z, :] = blocks[a * 16 : (a + 1) * 16]

    repeat(2, grad_rows)

    pltpu.make_async_remote_copy(
        src_ref=grad_blocks.at[1 - c],
        dst_ref=from_core,
        send_sem=send_sem.at[6],
        recv_sem=recv_sem.at[6],
        device_id=(z, x, 1 - c, y),
        device_id_type=MESH,
    ).start()


    def last(i):
        rows = rows_of(i, 256)
        layer_out[rows, :] = dot(p_second[rows, :], weights[1]).astype(BF16)

    repeat(4, last)
    store_layer = pltpu.make_async_copy(layer_out, layer_out_hbm, store_sem.at[2])
    store_layer.start()

    total_of(6, from_core).wait_recv()

    def add_core(i):
        four = pl.ds(i * 4, 4)
        core_sum[four] = (grad_blocks[c, four].astype(F32) + from_core[four].astype(F32)).astype(BF16)

    repeat(4, add_core)
    for step in range(1, NX * NY):
        px, py = across(step)
        pltpu.make_async_remote_copy(
            src_ref=core_sum.at[px * NY + py],
            dst_ref=from_across.at[step - 1],
            send_sem=send_sem.at[7],
            recv_sem=recv_sem.at[7],
            device_id=(z, px, c, py),
            device_id_type=MESH,
        ).start()
    send_pieces(5, feature_send, fresh_features_hbm, 1, 12)
    total_of(7, from_across).wait_recv()
    across_total = core_sum[column].astype(F32)
    for k in range(NX * NY - 1):
        across_total = across_total + from_across[k].astype(F32)
    across_sum[...] = across_total.astype(BF16)
    from_z[rows_of(z, 16), :] = across_sum[rows_of(z, 16), :]
    for k in range(1, NZ):
        pz = (z + k) % NZ
        pltpu.make_async_remote_copy(
            src_ref=across_sum.at[rows_of(pz, 16)],
            dst_ref=from_z.at[rows_of(z, 16)],
            send_sem=send_sem.at[8],
            recv_sem=recv_sem.at[8],
            device_id=(pz, x, c, y),
            device_id_type=MESH,
        ).start()
    send_pieces(5, feature_send, fresh_features_hbm, 12, 24)
    total_of(8, from_z.at[pl.ds(0, 112)]).wait_recv()
    total = from_z[0:16, :].astype(F32)
    for k in range(1, NZ):
        total = total + from_z[k * 16 : (k + 1) * 16, :].astype(F32)
    grads = total / TOTAL_NODES
    moment_new = decay_first * rows_f32[1] + (1.0 - decay_first) * grads
    second_new = decay_second * rows_f32[2] + (1.0 - decay_second) * grads * grads
    update = (
        moment_new
        / (1.0 - decay_first**STEP)
        / (jnp.sqrt(second_new / (1.0 - decay_second**STEP)) + epsilon)
    )
    master_next = rows_f32[0] - learn_rate * update
    rows_f32[3] = master_next
    shard_next[...] = master_next.astype(BF16)
    spread_shard(9, shard_next, gather_next)
    send_pieces(5, feature_send, fresh_features_hbm, 24, 34)
    for m in range(2):
        for r in range(2):
            for j in range(4):
                s = m * 8 + r * 4 + j
                master_next_ref[m, r : r + 1, j * 128 : (j + 1) * 128] = rows_f32[3, s : s + 1, :]
    gather_across(9, gather_next)
    send_pieces(5, feature_send, fresh_features_hbm, 34, 50)
    gather_core(9, gather_next)
    send_pieces(5, feature_send, fresh_features_hbm, 50, 64)
    gather_end(9, gather_next, weights_next)
    store_weights = pltpu.make_async_copy(weights_next, weights_next_hbm, store_sem.at[3])
    store_weights.start()

    for slot, gathered in ((0, gather_now), (9, gather_next)):
        total_of(slot, gathered.at[0, 0, pl.ds(0, 112)]).wait_send()
        total_of(slot + 1, gathered.at[0, pl.ds(0, 15)]).wait_send()
        total_of(slot + 2, gathered.at[0]).wait_send()
    total_of(6, from_core).wait_send()
    total_of(7, from_across).wait_send()
    total_of(8, from_z.at[pl.ds(0, 112)]).wait_send()
    for slot, source in ((3, raw_send), (4, grad_send), (5, feature_send)):
        total_of(slot, source.at[sent_bytes]).wait_send()
    total_of(4, fresh_grads_hbm.at[sent_bytes]).wait_recv()
    total_of(5, fresh_features_hbm.at[sent_bytes]).wait_recv()
    own_grads.wait()
    own_features.wait()
    store_layer.wait()
    store_weights.wait()


def deliver(*refs):
    sources, targets, held, sems = refs[:5], refs[5:10], refs[10:15], refs[15]
    steps = [
        (s.at[part], t.at[part], h.at[part])
        for s, t, h in zip(sources, targets, held)
        for part in (
            [pl.ds(0, 2)] if s.shape[0] == 2 else [pl.ds(k * 256, 256) for k in range(4)]
        )
    ]
    into = [pltpu.make_async_copy(s, h, sems.at[i]) for i, (s, t, h) in enumerate(steps)]
    out = [pltpu.make_async_copy(h, t, sems.at[i]) for i, (s, t, h) in enumerate(steps)]
    for copy in into:
        copy.start()
    for first, second in zip(into, out):
        first.wait()
        second.start()
    for copy in out:
        copy.wait()


def per_device(
    features,
    tile_src,
    tile_val,
    send_sel,
    stale_features,
    stale_grads,
    out_grad,
    master,
    moment_first,
    moment_second,
):
    any_space = pl.BlockSpec(memory_space=pl.ANY)
    vmem = pl.BlockSpec(memory_space=pltpu.VMEM)
    nodes = pltpu.VMEM((NODES, F), BF16)
    nodes_f32 = pltpu.VMEM((NODES, F), F32)
    matrices = pltpu.VMEM((2, F, F), BF16)
    blocks = pltpu.VMEM((2, NX * NY, 128, 128), BF16)
    half = pltpu.VMEM((NX * NY, 128, 128), BF16)
    lines = pltpu.VMEM((128, 128), BF16)
    shard = pltpu.VMEM((16, 128), BF16)
    square = pltpu.VMEM((256, 256), BF16)
    rows = jax.ShapeDtypeStruct((NODES, F), BF16)
    shapes = (
        rows,
        rows,
        rows,
        jax.ShapeDtypeStruct((2, 2, F), F32),
        jax.ShapeDtypeStruct((2, F, F), BF16),
    )
    made = pl.pallas_call(
        kernel,
        out_shape=shapes,
        in_specs=[vmem, vmem, vmem, vmem, vmem] + [any_space] * 5,
        out_specs=(any_space, any_space, any_space, vmem, any_space),
        scratch_shapes=[
            nodes,
            nodes,
            pltpu.VMEM((8, 8, 128, 128), BF16),
            pltpu.VMEM((NODES, 2 * NODES), BF16),
            pltpu.VMEM((NODES, 2 * NODES), BF16),
            nodes,
            nodes,
            nodes,
            nodes,
            nodes,
            nodes,
            pltpu.VMEM((F, NODES), BF16),
            nodes_f32,
            nodes_f32,
            nodes_f32,
            nodes,
            nodes,
            nodes,
            nodes,
            nodes,
            matrices,
            matrices,
            blocks,
            blocks,
            blocks,
            half,
            half,
            pltpu.VMEM((NX * NY - 1, 128, 128), BF16),
            lines,
            lines,
            shard,
            shard,
            pltpu.VMEM((4, 16, 128), F32),
            pltpu.VMEM((64, 1024), F32),
            pltpu.VMEM((NODES, 128), jnp.int32),
            pltpu.VMEM((NODES, NODES), BF16),
            square,
            square,
            pltpu.SemaphoreType.DMA((5,)),
            pltpu.SemaphoreType.DMA((4,)),
            pltpu.SemaphoreType.DMA((12,)),
            pltpu.SemaphoreType.DMA((12,)),
        ],
        compiler_params=pltpu.CompilerParams(
            collective_id=0, has_side_effects=True, vmem_limit_bytes=56 * 2**20
        ),
        cost_estimate=pl.CostEstimate(
            flops=12 * 2**30, bytes_accessed=12 * 2**20, transcendentals=2**20
        ),
    )(
        tile_src,
        send_sel,
        master,
        moment_first,
        moment_second,
        features,
        tile_val,
        stale_features,
        stale_grads,
        out_grad,
    )
    return pl.pallas_call(
        deliver,
        out_shape=shapes,
        in_specs=[any_space] * 5,
        out_specs=(any_space,) * 5,
        scratch_shapes=[pltpu.VMEM(shape.shape, shape.dtype) for shape in shapes]
        + [pltpu.SemaphoreType.DMA((14,))],
    )(*made)


def solution(mesh):
    torus = Mesh(mesh.devices.reshape(NZ, NX, NC, NY), DEVICES)
    nodes = P(DEVICES, None)
    parts = P(None, DEVICES, None)
    return jax.shard_map(
        per_device,
        mesh=torus,
        in_specs=(
            nodes,
            nodes,
            P(DEVICES, None, None, None),
            nodes,
            nodes,
            nodes,
            nodes,
            parts,
            parts,
            parts,
        ),
        out_specs=(nodes, nodes, nodes, parts, P()),
        check_vma=False,
    )
```

```python
import functools

import jax
import jax.numpy as jnp
from jax import lax
from jax.experimental import pallas as pl
from jax.experimental.pallas import tpu as pltpu
from jax.sharding import Mesh
from jax.sharding import PartitionSpec as P

STEP = 10
DEVICES = ("z", "x", "c", "y")
NZ, NX, NC, NY = 8, 4, 2, 4
PEERS = NZ * NX * NC
F = 512
NODES = 1024
PIECE = 16
TOTAL_NODES = 262144
MESH = pl.DeviceIdType.MESH
BF16 = jnp.bfloat16
F32 = jnp.float32

decay_first = 0.9
decay_second = 0.95
learn_rate = 0.01
epsilon = 1e-08


def dot(a, b):
    return jnp.dot(a, b, preferred_element_type=F32)


def dot_over_rows(a, b):
    return lax.dot_general(a, b, (((0,), (0,)), ((), ())), preferred_element_type=F32)


def dot_over_columns(a, b):
    return lax.dot_general(a, b, (((1,), (1,)), ((), ())), preferred_element_type=F32)


def rows_of(index, count):
    return pl.ds(pl.multiple_of(index * count, count), count)


def repeat(count, body):
    def step(i, carry):
        body(i)
        return carry

    lax.fori_loop(0, count, step, 0)


def kernel(
    src_ref,
    sel_row_ref,
    master_ref,
    first_ref,
    second_ref,
    features_hbm,
    tiles_hbm,
    stale_features_hbm,
    stale_grads_hbm,
    out_grad_hbm,
    layer_out_hbm,
    fresh_features_hbm,
    fresh_grads_hbm,
    master_next_ref,
    weights_next_hbm,
    features,
    rim,
    tiles,
    dense,
    dense_low,
    out_grad,
    stale_features,
    stale_grads,
    raw_send,
    feature_send,
    grad_send,
    upstream,
    p_local,
    p_stale,
    d_first,
    p_first,
    dz,
    hidden,
    p_second,
    layer_out,
    weights,
    weights_next,
    gather_now,
    gather_next,
    grad_blocks,
    from_core,
    core_sum,
    from_across,
    across_sum,
    from_z,
    shard_now,
    shard_next,
    rows_f32,
    src_wide,
    want_down,
    choose,
    perm,
    perm_back,
    load_sem,
    store_sem,
    send_sem,
    recv_sem,
):
    z, x, c, y = (lax.axis_index(a) for a in DEVICES)
    column = x * NY + y
    me = (z * NX + x) * NC + c

    loads = [
        pltpu.make_async_copy(s, d, load_sem.at[i])
        for i, (s, d) in enumerate(
            (
                (features_hbm, features),
                (tiles_hbm, tiles),
                (out_grad_hbm, out_grad),
                (stale_grads_hbm, stale_grads),
                (stale_features_hbm, stale_features),
            )
        )
    ]
    for load in loads:
        load.start()

    def peer_at(step):
        turn, dx_, dc_ = step % 8, (step // 8) % 4, step // 32
        half = (turn + 1) // 2
        dz_ = half * (turn % 2) + (NZ - half) * (1 - turn % 2)
        return ((z + dz_) % NZ, (x + dx_) % NX, (c + dc_) % NC)

    def across(step):
        return ((x + step // NY) % NX, (y + step % NY) % NY)

    barrier = pltpu.get_barrier_semaphore()

    def greet(i):
        pz, px, pc = peer_at(i + 1)
        pl.semaphore_signal(barrier, inc=1, device_id=(pz, px, pc, y), device_id_type=MESH)

    repeat(PEERS - 1, greet)
    for step in range(1, NX * NY):
        if step % NY:
            px, py = across(step)
            pl.semaphore_signal(barrier, inc=1, device_id=(z, px, c, py), device_id_type=MESH)

    def fill_rows(target, source):
        for m in range(2):
            for r in range(2):
                for j in range(4):
                    s = m * 8 + r * 4 + j
                    target[s : s + 1, :] = source[m, r : r + 1, j * 128 : (j + 1) * 128]

    fill_rows(rows_f32.at[0], master_ref)
    fill_rows(rows_f32.at[1], first_ref)
    fill_rows(rows_f32.at[2], second_ref)
    shard_now[...] = rows_f32[0].astype(BF16)

    def bits(o):
        m, j, p = o >> 7, (o >> 5) & 3, (o >> 4) & 1
        return (((o >> 3) & 1) << 7) | (p << 6) | (((o >> 1) & 3) << 4) | (m << 3) | ((o & 1) << 2) | j

    down = lax.broadcasted_iota(jnp.int32, (256, 256), 0)
    along = lax.broadcasted_iota(jnp.int32, (256, 256), 1)
    perm[...] = (bits(down) == along).astype(F32).astype(BF16)
    perm_back[...] = (bits(along) == down).astype(F32).astype(BF16)

    slot_of = lax.broadcasted_iota(jnp.int32, (PEERS, NODES), 1) // PIECE
    slot_at = lax.broadcasted_iota(jnp.int32, (PEERS, NODES), 0)
    widen = (slot_of == slot_at).astype(F32).astype(BF16)
    picks = jnp.broadcast_to(sel_row_ref[...].astype(F32), (16, PEERS)).astype(BF16)
    wide = dot(picks, widen)[0:1, :].astype(jnp.int32)
    lane = lax.broadcasted_iota(jnp.int32, (1, NODES), 1) % PIECE
    wanted = wide * PIECE + lane

    tall = dot_over_rows(widen, dot_over_rows(picks, jnp.full((16, 128), 0.0625, BF16)).astype(BF16))
    want_down[...] = tall.astype(jnp.int32) * PIECE + (
        lax.broadcasted_iota(jnp.int32, (NODES, 128), 0) % PIECE
    )

    def choose_rows(i):
        rows = rows_of(i, 256)
        for k in range(8):
            column = lax.broadcasted_iota(jnp.int32, (256, 128), 1) + k * 128
            chosen = (want_down[rows, :] == column).astype(F32).astype(BF16)
            choose[rows, k * 128 : (k + 1) * 128] = chosen

    repeat(4, choose_rows)

    pl.semaphore_wait(barrier, PEERS - 1 + NX * (NY - 1))

    def spread_shard(slot, shard, gathered):
        gathered[c, column, rows_of(z, 16), :] = shard[...]
        for k in range(1, NZ):
            pltpu.make_async_remote_copy(
                src_ref=shard,
                dst_ref=gathered.at[c, column, rows_of(z, 16)],
                send_sem=send_sem.at[slot],
                recv_sem=recv_sem.at[slot],
                device_id=((z + k) % NZ, x, c, y),
                device_id_type=MESH,
            ).start()

    def total_of(slot, ref):
        return pltpu.make_async_remote_copy(
            src_ref=ref,
            dst_ref=ref,
            send_sem=send_sem.at[slot],
            recv_sem=recv_sem.at[slot],
            device_id=(z, x, c, (y + 1) % NY),
            device_id_type=MESH,
        )

    def gather_across(slot, gathered):
        total_of(slot, gathered.at[0, 0, pl.ds(0, 112)]).wait_recv()
        for step in range(1, NX * NY):
            px, py = across(step)
            pltpu.make_async_remote_copy(
                src_ref=gathered.at[c, column],
                dst_ref=gathered.at[c, column],
                send_sem=send_sem.at[slot + 1],
                recv_sem=recv_sem.at[slot + 1],
                device_id=(z, px, c, py),
                device_id_type=MESH,
            ).start()

    def gather_core(slot, gathered):
        total_of(slot + 1, gathered.at[0, pl.ds(0, 15)]).wait_recv()
        pltpu.make_async_remote_copy(
            src_ref=gathered.at[c],
            dst_ref=gathered.at[c],
            send_sem=send_sem.at[slot + 2],
            recv_sem=recv_sem.at[slot + 2],
            device_id=(z, x, 1 - c, y),
            device_id_type=MESH,
        ).start()

    def gather_end(slot, gathered, whole):
        total_of(slot + 2, gathered.at[0]).wait_recv()

        def lay(group):
            taken = jnp.concatenate(
                [
                    jnp.concatenate(
                        [
                            gathered[a // 8, (k % 2) * 8 + a % 8, rows_of(group * 2 + k // 2, 16), :]
                            for a in range(16)
                        ],
                        0,
                    )
                    for k in range(4)
                ],
                1,
            )
            laid = dot(perm[...], taken).astype(BF16)
            for k in range(4):
                rows = rows_of(group * 4 + k, 32)
                for m in range(2):
                    for j in range(4):
                        at = (m * 4 + j) * 32
                        whole[m, rows, j * 128 : (j + 1) * 128] = laid[
                            at : at + 32, k * 128 : (k + 1) * 128
                        ]

        repeat(4, lay)

    def pick_pieces(target, table):
        def pick(i):
            rows = rows_of(i, 256)
            target[rows, :] = dot(choose[rows, :], table[...]).astype(BF16)

        repeat(4, pick)

    def send_pieces(slot, source, target, begin, end):
        def send(i):
            pz, px, pc = peer_at(i + begin)
            peer = (pz * NX + px) * NC + pc
            pltpu.make_async_remote_copy(
                src_ref=source.at[rows_of(peer, PIECE)],
                dst_ref=target.at[rows_of(me, PIECE)],
                send_sem=send_sem.at[slot],
                recv_sem=recv_sem.at[slot],
                device_id=(pz, px, pc, y),
                device_id_type=MESH,
            ).start()

        repeat(end - begin, send)

    sent_bytes = pl.ds(0, (PEERS - 1) * PIECE)

    spread_shard(0, shard_now, gather_now)
    loads[0].wait()
    pick_pieces(raw_send, features)
    send_pieces(3, raw_send, rim, 1, 24)
    rim[rows_of(me, PIECE), :] = raw_send[rows_of(me, PIECE), :]

    tile_of = lax.broadcasted_iota(jnp.int32, (8, 1024), 1) // 128
    tile_at = lax.broadcasted_iota(jnp.int32, (8, 1024), 0)
    wide_ids = dot(src_ref[...].astype(F32), (tile_of == tile_at).astype(F32))
    for i in range(8):
        src_wide[i * 8 : (i + 1) * 8, :] = jnp.broadcast_to(wide_ids[i : i + 1, :], (8, 1024))
    loads[1].wait()

    def densify(i):
        def column(b):
            target = jnp.full((8, 128), b, jnp.int32).astype(F32)
            total = jnp.zeros((128, 128), F32)
            for t in range(8):
                ids = src_wide[rows_of(i, 8), t * 128 : (t + 1) * 128]
                chosen = (ids == target).astype(F32)[0:1, :]
                total = total + tiles[i, t].astype(F32) * chosen
            high = total.astype(BF16)
            dense[rows_of(i, 128), rows_of(b, 128)] = high
            dense_low[rows_of(i, 128), rows_of(b, 128)] = (total - high.astype(F32)).astype(BF16)

        repeat(16, column)

    repeat(1, densify)
    gather_across(0, gather_now)
    send_pieces(3, raw_send, rim, 24, 64)
    repeat(3, lambda i: densify(i + 1))
    gather_core(0, gather_now)
    repeat(4, lambda i: densify(i + 4))

    loads[2].wait()
    loads[4].wait()
    loads[3].wait()

    def tiles_on(rows, columns, table):
        return dot(dense[rows, columns], table) + dot(dense_low[rows, columns], table)

    def ahead(i):
        rows = rows_of(i, 256)
        row = lax.broadcasted_iota(jnp.int32, (256, NODES), 0) + i * 256
        placing = (row == wanted).astype(F32).astype(BF16)
        d_first[rows, :] = dot(placing, stale_grads[...])
        p_local[rows, :] = tiles_on(rows, slice(0, NODES), features[...])
        p_stale[rows, :] = tiles_on(rows, slice(NODES, 2 * NODES), stale_features[...])

    repeat(4, ahead)

    gather_end(0, gather_now, weights)

    def tiles_back(columns):
        return dot(upstream[...], dense[:, columns]) + dot(upstream[...], dense_low[:, columns])

    def up(i):
        rows = rows_of(i, 256)
        upstream[:, rows] = dot_over_columns(weights[1], out_grad[rows, :]).astype(BF16)

    repeat(4, up)

    def rim_part(i):
        part = tiles_back(rows_of(i + 4, 256))
        grad_send[rows_of(i, 256), :] = part.astype(BF16).T

    repeat(4, rim_part)
    send_pieces(4, grad_send, fresh_grads_hbm, 1, 48)
    own_grads = pltpu.make_async_copy(
        grad_send.at[rows_of(me, PIECE)], fresh_grads_hbm.at[rows_of(me, PIECE)], store_sem.at[0]
    )
    own_grads.start()

    def local_part(i):
        rows = rows_of(i, 256)
        d_first[rows, :] += tiles_back(rows).T

    repeat(4, local_part)


    total_of(3, rim.at[sent_bytes]).wait_recv()

    def first_layer(i):
        rows = rows_of(i, 256)
        p = (p_local[rows, :] + tiles_on(rows, slice(NODES, 2 * NODES), rim[...])).astype(BF16)
        p_first[rows, :] = p
        zf = dot(p, weights[0])
        s = 1.0 / (1.0 + jnp.exp(-zf))
        hidden[rows, :] = (zf * s).astype(BF16)
        dz[rows, :] = (d_first[rows, :] * s * (1.0 + zf * (1.0 - s))).astype(BF16)

    repeat(4, first_layer)
    send_pieces(4, grad_send, fresh_grads_hbm, 48, 64)
    def second_layer(i):
        rows = rows_of(i, 256)
        p_second[rows, :] = (p_stale[rows, :] + tiles_on(rows, slice(0, NODES), hidden[...])).astype(BF16)

    repeat(4, second_layer)

    def grad_rows(i):
        chunk = 8
        first = dot_over_rows(p_first[:, rows_of(i, 256)], dz[...]).astype(BF16)
        second = dot_over_rows(p_second[:, rows_of(i, 256)], out_grad[...]).astype(BF16)
        for k in range(chunk):
            stacked = jnp.concatenate(
                [
                    g[k * 32 : (k + 1) * 32, j * 128 : (j + 1) * 128]
                    for g in (first, second)
                    for j in range(4)
                ],
                0,
            )
            blocks = dot(perm_back[...], stacked).astype(BF16)
            at_z, pair = rows_of(i * 4 + k // 2, 16), (k % 2) * 8
            for a in range(16):
                grad_blocks[a // 8, pair + a % 8, at_z, :] = blocks[a * 16 : (a + 1) * 16]

    repeat(2, grad_rows)

    pltpu.make_async_remote_copy(
        src_ref=grad_blocks.at[1 - c],
        dst_ref=from_core,
        send_sem=send_sem.at[6],
        recv_sem=recv_sem.at[6],
        device_id=(z, x, 1 - c, y),
        device_id_type=MESH,
    ).start()


    total_of(6, from_core).wait_recv()

    def add_core(i):
        four = pl.ds(i * 4, 4)
        core_sum[four] = (grad_blocks[c, four].astype(F32) + from_core[four].astype(F32)).astype(BF16)

    repeat(4, add_core)
    for step in range(1, NX * NY):
        px, py = across(step)
        pltpu.make_async_remote_copy(
            src_ref=core_sum.at[px * NY + py],
            dst_ref=from_across.at[step - 1],
            send_sem=send_sem.at[7],
            recv_sem=recv_sem.at[7],
            device_id=(z, px, c, py),
            device_id_type=MESH,
        ).start()
    pick_pieces(feature_send, hidden)
    send_pieces(5, feature_send, fresh_features_hbm, 1, 12)
    own_features = pltpu.make_async_copy(
        feature_send.at[rows_of(me, PIECE)],
        fresh_features_hbm.at[rows_of(me, PIECE)],
        store_sem.at[1],
    )
    own_features.start()

    def last(i):
        rows = rows_of(i, 256)
        layer_out[rows, :] = dot(p_second[rows, :], weights[1]).astype(BF16)

    repeat(4, last)
    store_layer = pltpu.make_async_copy(layer_out, layer_out_hbm, store_sem.at[2])
    store_layer.start()
    total_of(7, from_across).wait_recv()
    across_total = core_sum[column].astype(F32)
    for k in range(NX * NY - 1):
        across_total = across_total + from_across[k].astype(F32)
    across_sum[...] = across_total.astype(BF16)
    from_z[rows_of(z, 16), :] = across_sum[rows_of(z, 16), :]
    for k in range(1, NZ):
        pz = (z + k) % NZ
        pltpu.make_async_remote_copy(
            src_ref=across_sum.at[rows_of(pz, 16)],
            dst_ref=from_z.at[rows_of(z, 16)],
            send_sem=send_sem.at[8],
            recv_sem=recv_sem.at[8],
            device_id=(pz, x, c, y),
            device_id_type=MESH,
        ).start()
    send_pieces(5, feature_send, fresh_features_hbm, 12, 24)
    total_of(8, from_z.at[pl.ds(0, 112)]).wait_recv()
    total = from_z[0:16, :].astype(F32)
    for k in range(1, NZ):
        total = total + from_z[k * 16 : (k + 1) * 16, :].astype(F32)
    grads = total / TOTAL_NODES
    moment_new = decay_first * rows_f32[1] + (1.0 - decay_first) * grads
    second_new = decay_second * rows_f32[2] + (1.0 - decay_second) * grads * grads
    update = (
        moment_new
        / (1.0 - decay_first**STEP)
        / (jnp.sqrt(second_new / (1.0 - decay_second**STEP)) + epsilon)
    )
    master_next = rows_f32[0] - learn_rate * update
    rows_f32[3] = master_next
    shard_next[...] = master_next.astype(BF16)
    spread_shard(9, shard_next, gather_next)
    send_pieces(5, feature_send, fresh_features_hbm, 24, 34)
    for m in range(2):
        for r in range(2):
            for j in range(4):
                s = m * 8 + r * 4 + j
                master_next_ref[m, r : r + 1, j * 128 : (j + 1) * 128] = rows_f32[3, s : s + 1, :]
    gather_across(9, gather_next)
    send_pieces(5, feature_send, fresh_features_hbm, 34, 50)
    gather_core(9, gather_next)
    send_pieces(5, feature_send, fresh_features_hbm, 50, 64)
    gather_end(9, gather_next, weights_next)
    store_weights = pltpu.make_async_copy(weights_next, weights_next_hbm, store_sem.at[3])
    store_weights.start()

    for slot, gathered in ((0, gather_now), (9, gather_next)):
        total_of(slot, gathered.at[0, 0, pl.ds(0, 112)]).wait_send()
        total_of(slot + 1, gathered.at[0, pl.ds(0, 15)]).wait_send()
        total_of(slot + 2, gathered.at[0]).wait_send()
    total_of(6, from_core).wait_send()
    total_of(7, from_across).wait_send()
    total_of(8, from_z.at[pl.ds(0, 112)]).wait_send()
    for slot, source in ((3, raw_send), (4, grad_send), (5, feature_send)):
        total_of(slot, source.at[sent_bytes]).wait_send()
    total_of(4, fresh_grads_hbm.at[sent_bytes]).wait_recv()
    total_of(5, fresh_features_hbm.at[sent_bytes]).wait_recv()
    own_grads.wait()
    own_features.wait()
    store_layer.wait()
    store_weights.wait()


def deliver(*refs):
    sources, targets, held, sems = refs[:5], refs[5:10], refs[10:15], refs[15]
    steps = [
        (s.at[part], t.at[part], h.at[part])
        for s, t, h in zip(sources, targets, held)
        for part in (
            [pl.ds(0, 2)] if s.shape[0] == 2 else [pl.ds(k * 256, 256) for k in range(4)]
        )
    ]
    into = [pltpu.make_async_copy(s, h, sems.at[i]) for i, (s, t, h) in enumerate(steps)]
    out = [pltpu.make_async_copy(h, t, sems.at[i]) for i, (s, t, h) in enumerate(steps)]
    for copy in into:
        copy.start()
    for first, second in zip(into, out):
        first.wait()
        second.start()
    for copy in out:
        copy.wait()


def per_device(
    features,
    tile_src,
    tile_val,
    send_sel,
    stale_features,
    stale_grads,
    out_grad,
    master,
    moment_first,
    moment_second,
):
    any_space = pl.BlockSpec(memory_space=pl.ANY)
    vmem = pl.BlockSpec(memory_space=pltpu.VMEM)
    nodes = pltpu.VMEM((NODES, F), BF16)
    nodes_f32 = pltpu.VMEM((NODES, F), F32)
    matrices = pltpu.VMEM((2, F, F), BF16)
    blocks = pltpu.VMEM((2, NX * NY, 128, 128), BF16)
    half = pltpu.VMEM((NX * NY, 128, 128), BF16)
    lines = pltpu.VMEM((128, 128), BF16)
    shard = pltpu.VMEM((16, 128), BF16)
    square = pltpu.VMEM((256, 256), BF16)
    rows = jax.ShapeDtypeStruct((NODES, F), BF16)
    shapes = (
        rows,
        rows,
        rows,
        jax.ShapeDtypeStruct((2, 2, F), F32),
        jax.ShapeDtypeStruct((2, F, F), BF16),
    )
    made = pl.pallas_call(
        kernel,
        out_shape=shapes,
        in_specs=[vmem, vmem, vmem, vmem, vmem] + [any_space] * 5,
        out_specs=(any_space, any_space, any_space, vmem, any_space),
        scratch_shapes=[
            nodes,
            nodes,
            pltpu.VMEM((8, 8, 128, 128), BF16),
            pltpu.VMEM((NODES, 2 * NODES), BF16),
            pltpu.VMEM((NODES, 2 * NODES), BF16),
            nodes,
            nodes,
            nodes,
            nodes,
            nodes,
            nodes,
            pltpu.VMEM((F, NODES), BF16),
            nodes_f32,
            nodes_f32,
            nodes_f32,
            nodes,
            nodes,
            nodes,
            nodes,
            nodes,
            matrices,
            matrices,
            blocks,
            blocks,
            blocks,
            half,
            half,
            pltpu.VMEM((NX * NY - 1, 128, 128), BF16),
            lines,
            lines,
            shard,
            shard,
            pltpu.VMEM((4, 16, 128), F32),
            pltpu.VMEM((64, 1024), F32),
            pltpu.VMEM((NODES, 128), jnp.int32),
            pltpu.VMEM((NODES, NODES), BF16),
            square,
            square,
            pltpu.SemaphoreType.DMA((5,)),
            pltpu.SemaphoreType.DMA((4,)),
            pltpu.SemaphoreType.DMA((12,)),
            pltpu.SemaphoreType.DMA((12,)),
        ],
        compiler_params=pltpu.CompilerParams(
            collective_id=0, has_side_effects=True, vmem_limit_bytes=56 * 2**20
        ),
        cost_estimate=pl.CostEstimate(
            flops=12 * 2**30, bytes_accessed=12 * 2**20, transcendentals=2**20
        ),
    )(
        tile_src,
        send_sel,
        master,
        moment_first,
        moment_second,
        features,
        tile_val,
        stale_features,
        stale_grads,
        out_grad,
    )
    return pl.pallas_call(
        deliver,
        out_shape=shapes,
        in_specs=[any_space] * 5,
        out_specs=(any_space,) * 5,
        scratch_shapes=[pltpu.VMEM(shape.shape, shape.dtype) for shape in shapes]
        + [pltpu.SemaphoreType.DMA((14,))],
    )(*made)


def solution(mesh):
    torus = Mesh(mesh.devices.reshape(NZ, NX, NC, NY), DEVICES)
    nodes = P(DEVICES, None)
    parts = P(None, DEVICES, None)
    return jax.shard_map(
        per_device,
        mesh=torus,
        in_specs=(
            nodes,
            nodes,
            P(DEVICES, None, None, None),
            nodes,
            nodes,
            nodes,
            nodes,
            parts,
            parts,
            parts,
        ),
        out_specs=(nodes, nodes, nodes, parts, P()),
        check_vma=False,
    )
```
